512 devices in a mesh: attn: 32 (over z, core), ffn: 4 (over x), rep: 4 (over y).
Axes of the slice: x: 4, y: 4, z: 16, core: 2. Of those that a mesh axis runs over, the one named last changes fastest.
Arguments:
- queries: bfloat16 [4, 128, 16384], P('rep', 'attn', 'ffn'), may hold values from -6 to 6
- keys: bfloat16 [4, 128, 256, 256], P('rep', 'attn'), may hold values from -6 to 6
- values: bfloat16 [4, 128, 256, 256], P('rep', 'attn'), may hold values from -6 to 6
- lengths: int32 [4, 128], P('rep', 'attn'), may hold values from 2 to 256
- out_proj: bfloat16 [7168, 16384], P('attn', 'ffn'), may hold values from -0.046875 to 0.046875
- residual: bfloat16 [4, 128, 7168], P('rep', 'ffn', 'attn'), may hold values from -6 to 6
- norm_gain: float32 [7168], P('attn'), may hold values from 0.1 to 1.9
- expert_ids: int32 [4, 128, 3], P('rep', 'ffn'), may hold values from 0 to 7, all different within a row; in each aligned block of 32 rows (0 to 31, 32 to 63, ..., all dimensions but the last counted through in order) at most 14 rows name the same one
- gate_weights: float32 [4, 128, 3], P('rep', 'ffn'), may hold values from 0.1 to 1
- w_gate: bfloat16 [8, 7168, 2560], P('ffn', 'attn', 'rep'), may hold values from -0.0625 to 0.0625
- w_up: bfloat16 [8, 7168, 2560], P('ffn', 'attn', 'rep'), may hold values from -0.0625 to 0.0625
- w_down: bfloat16 [8, 7168, 2560], P('ffn', 'attn', 'rep'), may hold values from -0.125 to 0.125
Outputs:
- mixed: float32 [4, 128, 7168], P('rep', 'ffn', 'attn')
The draws below stay inside these ranges and needn't reach their ends.
Inputs may be any that keep to these rules, and one draw needn't show every extreme that they name: `expert_ids`: each row names 3 different experts. In each aligned block of 32 rows of one batch, no expert is named by more than 14 rows, a bound that some block reaches.
All inputs are finite; a program needn't handle non-finite values.
Results may differ from the reference program's by a relative error of at most 0.007.
Values may be sent and summed in bfloat16 or wider, within the bound.
A program may use at most 64 MiB of HBM per device.

```python
import math
import jax
import jax.numpy as jnp
import numpy as np
from jax import lax

D = 7168
HEADS = 64
HD = 256
TOP = 3
EFF = 2560
CTX = 256
R = 128
QROWS = 32
CAP = 14
EXPERTS = 8
N_REP = 4


def draw_queries(key, part):
    base_key = jax.random.fold_in(key, 11)
    drawn = jax.random.truncated_normal(base_key, -6.0, 6.0, (N_REP, R, HEADS * HD), jnp.float32)
    return drawn.astype(jnp.bfloat16)


def draw_keys(key, part):
    base_key = jax.random.fold_in(key, 12)
    drawn = jax.random.truncated_normal(base_key, -6.0, 6.0, (N_REP, R, CTX, HD), jnp.float32)
    return drawn.astype(jnp.bfloat16)


def place_ends(values, own_key, low, top_value):
    shape = values.shape
    spot = [jax.random.randint(jax.random.fold_in(own_key, axis), (), 0, shape[axis]) for axis in range(len(shape))]
    values = values.at[tuple(spot)].set(low)
    longest = shape.index(max(shape))
    spot[longest] = (spot[longest] + 1) % shape[longest]
    return values.at[tuple(spot)].set(top_value)


def shard_levels(key, shape, cuts, least, high):
    gain = 1.0
    for dim, parts in cuts:
        draws = jax.random.uniform(jax.random.fold_in(jax.random.fold_in(key, 6), dim), (parts,), jnp.float32, least / len(cuts), high / len(cuts))
        gain = gain * jnp.repeat(jnp.exp(draws), shape[dim] // parts).reshape((-1,) + (1,) * (len(shape) - 1 - dim))
    return gain


def assign_block(stream_key, own, number, rows, count, top, bound, slope):
    ranking = jax.random.permutation(stream_key, count)
    heavy_load, ordinary = load_shares(count, rows * top, bound, slope, True), load_shares(count, rows * top, bound, slope, False)
    places = jnp.arange(count)

    def named(sizes, rotation):
        used = int((sizes > 0).sum())
        fixed = max(1, used // 4)
        passed = fixed + (places - fixed + rotation * (used - fixed)) % max(1, count - fixed)
        return jnp.zeros((count,), jnp.int32).at[ranking[jnp.where(places < fixed, places, passed)]].set(jnp.asarray(sizes, jnp.int32))

    sizes = jnp.where(number % 4 == 0, named(heavy_load, number // 4), named(ordinary, number - number // 4 - 1))
    mixed = jax.random.permutation(jax.random.fold_in(own, 3), count)
    donor, taker = mixed[0:count // 2 * 2:2], mixed[1:count // 2 * 2:2]
    room = jnp.minimum(sizes[donor] - 1, bound - sizes[taker]) // 2
    room = jnp.where((donor == ranking[0]) | (taker == ranking[0]) | (sizes[taker] == 0), 0, jnp.maximum(room, 0))
    passed = jax.random.randint(jax.random.fold_in(own, 4), (count // 2,), 0, 1 << 20) % (room + 1)
    sizes = sizes.at[donor].add(-passed).at[taker].add(passed)
    members = jnp.searchsorted(jnp.cumsum(sizes), jnp.arange(rows * top), side="right").astype(jnp.int32)
    table = members.reshape(top, rows).T
    table = table[jax.random.permutation(jax.random.fold_in(own, 1), rows)]
    rotation = jax.random.randint(jax.random.fold_in(own, 2), (rows, 1), 0, top)
    return jnp.take_along_axis(table, (jnp.arange(top)[None, :] + rotation) % top, axis=1)


def load_shares(amount, total, reach, slope, full):
    loads = [(1 << 20) // math.isqrt(standing ** slope) + 1 for standing in range(1, amount + 1)]
    largest = reach if full else min(reach, max(-(-total // amount), total * loads[0] // sum(loads)))
    least = 1 if total - largest >= amount - 1 else 0
    counts, rest = [largest] + [least] * (amount - 1), total - largest - least * (amount - 1)
    while rest > 0:
        movable = [i for i in range(1, amount) if counts[i] < largest] or [i for i in range(1, amount) if counts[i] < reach]
        whole, left = sum([loads[i] for i in movable]), rest
        for i in movable:
            extra = min(reach - counts[i], max(1, left * loads[i] // whole), rest)
            counts[i] = counts[i] + extra
            rest = rest - extra
    return np.array(counts)


def bell_draw(key, dims, deviation, reach, pieces=(), held_as=jnp.bfloat16):
    values = deviation * jax.random.normal(key, dims, jnp.float32)
    if pieces:
        values = values * shard_levels(key, dims, pieces, -0.22, 0.18)
    return jnp.clip(values, -reach, reach).astype(held_as)


def setup_inputs(seed: int = 0) -> dict:
    splits = jax.random.split(jax.random.key(seed), 13)
    queries = draw_queries(jax.random.fold_in(splits[12], 71), 0)
    keys = draw_keys(jax.random.fold_in(splits[12], 71), 0)
    values = bell_draw(splits[2], (N_REP, R, CTX, HD), 1.0, 6.0, ((0, 4), (1, 32)))
    lengths = place_ends(jax.random.randint(splits[3], (N_REP, R), 2, CTX + 1), jax.random.fold_in(splits[3], 1), 2, CTX).astype(jnp.int32)
    out_proj = bell_draw(splits[4], (D, HEADS * HD), (HEADS * HD) ** -0.5, 0.046875, ((0, 32), (1, 4)))
    residual = bell_draw(splits[5], (N_REP, R, D), 1.0, 6.0, ((0, 4), (1, 4), (2, 32)))
    norm_gain = jnp.clip(1.0 + 0.18 * jax.random.normal(splits[6], (D,), jnp.float32), 0.1, 1.9)
    expert_ids_keys = jax.random.split(jax.random.fold_in(splits[7], 1), N_REP * R // QROWS)
    expert_ids_turns = jax.random.permutation(jax.random.fold_in(splits[7], 3), N_REP * R // QROWS)
    expert_ids = jax.vmap(lambda own, number: assign_block(jax.random.fold_in(splits[7], 2), own, number, QROWS, EXPERTS, TOP, CAP, 2))(expert_ids_keys, expert_ids_turns).reshape((N_REP, R, TOP))
    gate_weights = jnp.clip(0.1 + 0.9 * jax.random.uniform(splits[8], (N_REP, R, TOP), jnp.float32) ** shard_levels(splits[8], (N_REP, R, TOP), ((0, 4), (1, 4)), -0.2, 0.2), 0.1, 1.0)
    w_gate = bell_draw(splits[9], (EXPERTS, D, EFF), D ** -0.5, 0.0625, ((0, 4), (1, 32), (2, 4)))
    w_up = bell_draw(splits[10], (EXPERTS, D, EFF), D ** -0.5, 0.0625, ((0, 4), (1, 32), (2, 4)))
    w_down = bell_draw(splits[11], (EXPERTS, D, EFF), EFF ** -0.5, 0.125, ((0, 4), (1, 32), (2, 4)))
    return dict(queries=queries, keys=keys, values=values, lengths=lengths, out_proj=out_proj, residual=residual, norm_gain=norm_gain, expert_ids=expert_ids, gate_weights=gate_weights, w_gate=w_gate, w_up=w_up, w_down=w_down)


def reference(queries, keys, values, lengths, out_proj, residual, norm_gain, expert_ids, gate_weights, w_gate, w_up, w_down):
    groups, requests, _ = queries.shape
    query_heads = queries.reshape(groups, requests, HEADS, HD).astype(jnp.float32)
    scores = jnp.einsum('grhd,grtd->grht', query_heads, keys.astype(jnp.float32)) * HD ** (-0.5)
    position = jnp.arange(CTX, dtype=jnp.int32)
    live = position[None, None, None, :] < lengths[:, :, None, None]
    scores = jnp.where(live, scores, jnp.float32(-1e+30))
    probs = jax.nn.softmax(scores, axis=-1).astype(jnp.bfloat16)
    attended = jnp.einsum('grht,grtd->grhd', probs.astype(jnp.float32), values.astype(jnp.float32))
    attended = attended.astype(jnp.bfloat16).reshape(groups * requests, HEADS * HD)
    projected = jnp.dot(attended, out_proj.T, preferred_element_type=jnp.float32)
    hidden = residual.reshape(groups * requests, D).astype(jnp.float32) + projected
    hidden_bf = hidden.astype(jnp.bfloat16).astype(jnp.float32)
    rinv = lax.rsqrt(lax.optimization_barrier(jnp.mean(hidden_bf * hidden_bf, axis=-1)) + 1e-06)
    normed = (hidden_bf * norm_gain).astype(jnp.bfloat16)
    chosen = (expert_ids[..., None] == jnp.arange(EXPERTS, dtype=jnp.int32)).astype(jnp.float32)
    shares = lax.optimization_barrier(jnp.sum(gate_weights[..., None] * chosen, axis=2)).reshape(groups * requests, EXPERTS)

    def expert_step(total, packed):
        weight_gate, weight_up, weight_down, share = packed
        gate_val = jnp.dot(normed, weight_gate, preferred_element_type=jnp.float32) * rinv[:, None]
        up_val = jnp.dot(normed, weight_up, preferred_element_type=jnp.float32) * rinv[:, None]
        activated = (jax.nn.silu(gate_val) * up_val).astype(jnp.bfloat16)
        expert_out = jnp.dot(activated, weight_down.T, preferred_element_type=jnp.float32)
        return (total + share[:, None] * expert_out, None)
    start = jnp.zeros((groups * requests, D), jnp.float32)
    moe_out, _ = lax.scan(expert_step, start, (w_gate, w_up, w_down, shares.T))
    return (hidden + moe_out).reshape(groups, requests, D)
```

```python
import functools

import jax
import jax.numpy as jnp
from jax import lax
from jax.experimental import pallas as pl
from jax.experimental.pallas import tpu as pltpu
from jax.sharding import PartitionSpec as P

MESH = pl.DeviceIdType.MESH
BF = jnp.bfloat16
F32 = jnp.float32
NT = (((1,), (1,)), ((), ()))
NN = (((1,), (0,)), ((), ()))

CHIPS = 16
SIDE = 4
W = 224
WP = 256
CAP = 14
SLOT = 16
ROWS = 32
EFF = 640
HD = 256
KH = 2048
D = 7168

PLANE = sorted(
    ((df, dr, dc) for df in range(4) for dr in range(4) for dc in range(2) if df or dr or dc),
    key=lambda o: (-(min(o[0], 4 - o[0]) + min(o[1], 4 - o[1])), o),
)
XCORE = sorted(
    ((df, dc) for df in range(4) for dc in range(2) if df or dc),
    key=lambda o: (-min(o[0], 4 - o[0]), o),
)


def mm(a, b, dims=NN):
    return lax.dot_general(a, b, dims, preferred_element_type=F32)


def kernel(
    q_h, k_h, v_h, len_h, wo_h, res_h, gain_h, ids_h, gw_h, wg_h, wu_h, wd_h,
    out_ref,
    qv, kv, vv, lenv, resv, gainv, idsv, gwv, wo, wg, wu, wd,
    qs, att, xs, xr, ag1, us, rb, pad32, pad1, tok, xb, pb, r1, ra, s2, r2, ag2, eb, rr,
    ld, ss, rs,
):
    a = lax.axis_index("attn")
    f = lax.axis_index("ffn")
    r = lax.axis_index("rep")
    c = lax.rem(a, 2)
    z = lax.div(a, 2)
    sg = 1 - 2 * c

    def zdev(d):
        return {"attn": lax.rem(z + d + CHIPS, CHIPS) * 2 + c}

    def zidx(d):
        return lax.rem(z + d + 2 * CHIPS, CHIPS)

    def pdev(o):
        df, dr, dc = o
        return {
            "attn": z * 2 + lax.rem(c + dc, 2),
            "ffn": lax.rem(f + df, 4),
            "rep": lax.rem(r + dr, 4),
        }

    sib = {"attn": z * 2 + 1 - c}

    loads = []

    def load(src, dst):
        cp = pltpu.make_async_copy(src, dst, ld.at[len(loads)])
        cp.start()
        loads.append(cp)
        return cp

    sent = []

    def send(src, dst, dev):
        k = len(sent)
        cp = pltpu.make_async_remote_copy(
            src_ref=src, dst_ref=dst, send_sem=ss.at[k], recv_sem=rs.at[k],
            device_id=dev, device_id_type=MESH,
        )
        cp.start()
        sent.append(cp)
        return cp

    l_q = load(q_h.at[0], qv)
    l_k = load(k_h.at[0], kv)
    l_v = load(v_h.at[0], vv)
    l_len = load(len_h, lenv)
    l_ids = load(ids_h.at[0], idsv)
    l_gw = load(gw_h.at[0], gwv)
    l_res = load(res_h.at[0], resv)
    l_gain = load(gain_h, gainv)

    barrier = pltpu.get_barrier_semaphore()
    peers = [pdev(o) for o in PLANE] + [zdev(d) for d in (6, -6, 3, -3, 2, -2, 1, -1)]
    for dev in peers:
        pl.semaphore_signal(barrier, inc=1, device_id=dev, device_id_type=MESH)

    half = pl.multiple_of(c * KH, KH)
    other = pl.multiple_of((1 - c) * KH, KH)
    l_wo = load(wo_h.at[:, pl.ds(half, KH)], wo.at[c, pl.ds(0, W)])
    l_wg = load(wg_h.at[c], wg.at[c, pl.ds(0, W)])
    l_wu = load(wu_h.at[c], wu.at[c, pl.ds(0, W)])
    l_wd = load(wd_h.at[c], wd.at[c, pl.ds(0, W)])

    l_q.wait()
    q32 = qv[...].astype(F32)
    for i in range(4):
        for h in range(16):
            qs[i * 16 + h : i * 16 + h + 1, :] = q32[i : i + 1, h * HD : (h + 1) * HD]
    l_k.wait()
    l_len.wait()
    l_v.wait()
    position = lax.broadcasted_iota(jnp.int32, (16, HD), 1)
    for i in range(4):
        s = mm(qs[i * 16 : (i + 1) * 16, :].astype(BF), kv[i], NT) * (HD**-0.5)
        s = jnp.where(position < lenv[0:1, i : i + 1], s, F32(-1e30))
        e = jnp.exp(s - jnp.max(s, axis=1, keepdims=True))
        p = (e / jnp.sum(e, axis=1, keepdims=True)).astype(BF)
        o = mm(p, vv[i])
        for h in range(16):
            hh, hg, j = h // 8, (h % 8) // 4, h % 4
            for k in range(2):
                row = hg * 8 + k * 4 + i
                att[hh, row : row + 1, j * HD : (j + 1) * HD] = o[h : h + 1, :]
    rowi = lax.broadcasted_iota(jnp.int32, (16, 1024), 0)
    mine = lax.rem(lax.div(rowi, 4), 2) == c
    xs[...] = jnp.where(mine, att[1 - c], 0.0).astype(BF)

    pl.semaphore_wait(barrier, len(peers))
    x_cp = send(xs, xr, sib)
    x_wo = send(wo_h.at[:, pl.ds(other, KH)], wo.at[c, pl.ds(0, W)], sib)
    x_wg = send(wg_h.at[1 - c], wg.at[c, pl.ds(0, W)], sib)
    x_wu = send(wu_h.at[1 - c], wu.at[c, pl.ds(0, W)], sib)
    x_wd = send(wd_h.at[1 - c], wd.at[c, pl.ds(0, W)], sib)

    def gather_z(buf):
        own = buf.at[z]
        first = {d: send(own, own, zdev(d)) for d in (6, -6, 3, -3, 1, -1)}
        rest = []
        first[6].wait_recv()
        far = buf.at[zidx(-6)]
        rest += [send(far, far, zdev(1)), send(far, far, zdev(-1))]
        first[-6].wait_recv()
        far = buf.at[zidx(6)]
        rest += [send(far, far, zdev(-1)), send(far, far, zdev(1))]
        far = buf.at[zidx(-6 * sg)]
        rest += [send(far, far, zdev(2 * sg))]
        first[3].wait_recv()
        far = buf.at[zidx(-3)]
        rest += [send(far, far, zdev(1)), send(far, far, zdev(-1))]
        first[-3].wait_recv()
        far = buf.at[zidx(3)]
        rest += [send(far, far, zdev(-1)), send(far, far, zdev(1))]
        return [first[1], first[-1]] + rest

    x_cp.wait_recv()
    ag1[z] = jnp.where(mine, att[c], 0.0).astype(BF) + xr[...]
    pending = gather_z(ag1)

    for buf in (wo, wg, wu, wd):
        buf[:, W:WP, :] = jnp.zeros((2, WP - W, buf.shape[2]), BF)
    l_res.wait()
    l_gain.wait()
    l_ids.wait()
    l_gw.wait()
    pad32[...] = jnp.zeros((ROWS, WP), F32)
    pad32[:, 0:W] = resv[...].astype(F32)
    pad1[...] = jnp.zeros((1, WP), F32)
    pad1[:, 0:W] = gainv[...]
    lane = lax.broadcasted_iota(jnp.int32, (ROWS, 128), 1)
    ids = idsv[...]
    gws = gwv[...]
    hits = jnp.zeros((ROWS, 128), F32)
    share = jnp.zeros((ROWS, 128), F32)
    for k in range(3):
        same = ids[:, k : k + 1] == lax.div(lane, SLOT)
        hits = hits + jnp.where(same, 1.0, 0.0)
        share = share + jnp.where(same, gws[:, k : k + 1], 0.0)
    lower = lax.broadcasted_iota(jnp.int32, (ROWS, ROWS), 0) > lax.broadcasted_iota(
        jnp.int32, (ROWS, ROWS), 1
    )
    before = mm(jnp.where(lower, 1.0, 0.0).astype(BF), hits.astype(BF))
    placed = before == lax.rem(lane, SLOT).astype(F32)
    pick_t = jnp.where(placed, hits, 0.0).astype(BF)
    share = jnp.where(placed, share, 0.0)
    eye = lax.broadcasted_iota(jnp.int32, (128, 128), 0) == lax.broadcasted_iota(
        jnp.int32, (128, 128), 1
    )
    pick = mm(jnp.where(eye, 1.0, 0.0).astype(BF), pick_t, NT).astype(BF)
    share_hi = share.astype(BF)
    share_lo = (share - share_hi.astype(F32)).astype(BF)
    share_hi = jnp.concatenate([share_hi] * 4, axis=1)
    share_lo = jnp.concatenate([share_lo] * 4, axis=1)

    l_wo.wait()
    x_wo.wait_recv()
    for cp in pending:
        cp.wait_recv()

    rows = ag1[...].reshape(CHIPS * 16, 1024)
    for s in range(2):
        p0 = mm(rows, wo[s, :, 0:1024], NT).reshape(CHIPS, 16, WP)
        p1 = mm(rows, wo[s, :, 1024:2048], NT).reshape(CHIPS, 16, WP)
        u = p0[:, 0:8] + p1[:, 8:16]
        us[s] = u.reshape(4, ROWS, WP).astype(BF)
    pending = []
    for df, dc in XCORE:
        q = lax.rem(f + df, 4)
        s = lax.rem(c + dc, 2)
        pending.append(send(us.at[s, q], rb.at[f * 2 + c], pdev((df, 0, dc))))
    rb[f * 2 + c] = us[c, f]
    hidden = pad32[...]
    for cp in pending:
        cp.wait_recv()
    for k in range(8):
        hidden = hidden + rb[k].astype(F32)
    hid = hidden.astype(BF).astype(F32)
    squares = jnp.sum(hid * hid, axis=1, keepdims=True)
    sq_hi = squares.astype(BF).astype(F32)
    lane2 = lax.broadcasted_iota(jnp.int32, (ROWS, WP), 1)
    normed = jnp.where(
        lane2 == W, sq_hi, jnp.where(lane2 == W + 1, squares - sq_hi, hid * pad1[...])
    ).astype(BF)
    tok[...] = mm(pick, normed).astype(BF).reshape(8, SLOT, WP)

    pending = []
    for o in PLANE:
        e = lax.rem(f + o[0], 4) * 2 + lax.rem(c + o[2], 2)
        pending.append(send(tok.at[e], xb.at[c, r * 4 + f], pdev(o)))
    xb[c, r * 4 + f] = tok[f * 2 + c]
    l_wg.wait()
    x_wg.wait_recv()
    l_wu.wait()
    x_wu.wait_recv()
    for cp in pending:
        cp.wait_recv()
    x0 = xb[0].reshape(256, WP)
    x1 = xb[1].reshape(256, WP)
    ones = lax.broadcasted_iota(jnp.int32, (16, WP), 1)
    ones = jnp.where((ones == W) | (ones == W + 1), 1.0, 0.0).astype(BF)
    sq = (mm(ones, x0, NT) + mm(ones, x1, NT))[0:1, :]
    sq_hi = sq.astype(BF).astype(F32)
    sq_lo = sq - sq_hi
    gate = mm(x0, wg[0]) + mm(x1, wg[1])
    slot = lax.rem(lax.broadcasted_iota(jnp.int32, (256, 256), 0), SLOT)
    head = jnp.where(slot == CAP, sq_hi, jnp.where(slot == CAP + 1, sq_lo, gate[:, 0:256]))
    pb[:, :, 0:256] = head.astype(BF).reshape(CHIPS, SLOT, 256)
    pb[:, :, 256:EFF] = gate[:, 256:EFF].astype(BF).reshape(CHIPS, SLOT, EFF - 256)
    up = mm(x0, wu[0]) + mm(x1, wu[1])
    pb[:, :, EFF : 2 * EFF] = up.astype(BF).reshape(CHIPS, SLOT, EFF)

    near = {}
    for k, (o, d) in enumerate(((7, -1), (5, 1))):
        for side, sgn in enumerate((1, -1)):
            near[side, k] = send(pb.at[zidx(-sgn * o)], r1.at[side, k], zdev(sgn * d))
    anti = send(pb.at[zidx(8)], ra, zdev(-2 * sg))
    for k, (o, d) in enumerate(((4, -1), (2, 1))):
        for side, sgn in enumerate((1, -1)):
            near[side, k + 2] = send(pb.at[zidx(-sgn * o)], r1.at[side, k + 2], zdev(sgn * d))
    pending = []
    for side, sgn in enumerate((1, -1)):
        near[side, 0].wait_recv()
        near[side, 1].wait_recv()
    anti.wait_recv()
    for side, sgn in enumerate((1, -1)):
        t = zidx(-sgn * 6)
        acc = pb[t].astype(F32) + r1[side, 0].astype(F32) + r1[side, 1].astype(F32)
        acc = acc + jnp.where(c == side, ra[...].astype(F32), 0.0)
        s2[side, 0] = acc.astype(BF)
        pending.append(send(s2.at[side, 0], r2.at[side, 0], zdev(-sgn * 6)))
    for side, sgn in enumerate((1, -1)):
        near[side, 2].wait_recv()
        near[side, 3].wait_recv()
        t = zidx(-sgn * 3)
        acc = pb[t].astype(F32) + r1[side, 2].astype(F32) + r1[side, 3].astype(F32)
        s2[side, 1] = acc.astype(BF)
        pending.append(send(s2.at[side, 1], r2.at[side, 1], zdev(-sgn * 3)))
    for side, sgn in enumerate((1, -1)):
        pending.append(send(pb.at[zidx(-sgn)], r2.at[side, 2], zdev(-sgn)))
    total = pb[z].astype(F32)
    for cp in pending:
        cp.wait_recv()
    for side in range(2):
        for k in range(3):
            total = total + r2[side, k].astype(F32)
    sq = total[CAP : CAP + 1, 0:256] + total[CAP + 1 : CAP + 2, 0:256]
    row = lax.broadcasted_iota(jnp.int32, (SLOT, 256), 0)
    lane3 = lax.broadcasted_iota(jnp.int32, (SLOT, 256), 1)
    sq = jnp.sum(jnp.where(lane3 == z * SLOT + row, sq, 0.0), axis=1, keepdims=True)
    rinv = lax.rsqrt(sq / D + 1e-6)
    gate = total[:, 0:EFF] * rinv
    up = total[:, EFF : 2 * EFF] * rinv
    act = gate / (1.0 + jnp.exp(-gate)) * up
    live = lax.broadcasted_iota(jnp.int32, (SLOT, EFF), 0) < CAP
    ag2[z] = jnp.where(live, act, 0.0).astype(BF)

    pending = gather_z(ag2)
    l_wd.wait()
    x_wd.wait_recv()
    for cp in pending:
        cp.wait_recv()
    rows = ag2[...].reshape(256, EFF)
    for s in range(2):
        eb[s] = mm(rows, wd[s], NT).astype(BF).reshape(16, SLOT, WP)

    pending = []
    for o in PLANE:
        b = lax.rem(r + o[1], 4) * 4 + lax.rem(f + o[0], 4)
        s = lax.rem(c + o[2], 2)
        pending.append(send(eb.at[s, b], rr.at[r * 8 + f * 2 + c], pdev(o)))
    rr[r * 8 + f * 2 + c] = eb[c, r * 4 + f]
    for cp in pending:
        cp.wait_recv()
    back = rr[...].reshape(512, WP)
    mixed = hidden + mm(share_hi, back) + mm(share_lo, back)
    out_ref[0] = mixed[:, 0:W]
    for cp in sent:
        cp.wait_send()


N_SENT = 5 + 15 + 7 + 31 + 9 + 6 + 15 + 31


def per_device(q, k, v, lens, wo, res, gain, ids, gw, wg, wu, wd):
    any_spec = pl.BlockSpec(memory_space=pl.ANY)
    vm = pltpu.VMEM
    dma = pltpu.SemaphoreType.DMA
    return pl.pallas_call(
        kernel,
        name="layer",
        out_shape=jax.ShapeDtypeStruct((1, ROWS, W), F32),
        in_specs=[any_spec] * 12,
        out_specs=pl.BlockSpec(memory_space=pltpu.VMEM),
        scratch_shapes=[
            vm((4, 4096), BF),
            vm((4, 256, HD), BF),
            vm((4, 256, HD), BF),
            vm((1, 4), jnp.int32),
            vm((ROWS, W), BF),
            vm((1, W), F32),
            vm((ROWS, 3), jnp.int32),
            vm((ROWS, 3), F32),
            vm((2, WP, KH), BF),
            vm((2, WP, EFF), BF),
            vm((2, WP, EFF), BF),
            vm((2, WP, EFF), BF),
            vm((64, HD), F32),
            vm((2, 16, 1024), F32),
            vm((16, 1024), BF),
            vm((16, 1024), BF),
            vm((CHIPS, 16, 1024), BF),
            vm((2, 4, ROWS, WP), BF),
            vm((8, ROWS, WP), BF),
            vm((ROWS, WP), F32),
            vm((1, WP), F32),
            vm((8, SLOT, WP), BF),
            vm((2, 16, SLOT, WP), BF),
            vm((CHIPS, SLOT, 2 * EFF), BF),
            vm((2, 4, SLOT, 2 * EFF), BF),
            vm((SLOT, 2 * EFF), BF),
            vm((2, 2, SLOT, 2 * EFF), BF),
            vm((2, 3, SLOT, 2 * EFF), BF),
            vm((CHIPS, SLOT, EFF), BF),
            vm((2, 16, SLOT, WP), BF),
            vm((32, SLOT, WP), BF),
            dma((12,)),
            dma((N_SENT,)),
            dma((N_SENT,)),
        ],
        compiler_params=pltpu.CompilerParams(
            collective_id=0, has_side_effects=True, vmem_limit_bytes=56 * 1024 * 1024
        ),
    )(q, k, v, lens, wo, res, gain.reshape(1, W), ids, gw, wg, wu, wd)


def solution(mesh):
    in_specs = (
        P("rep", "attn", "ffn"),
        P("rep", "attn", None, None),
        P("rep", "attn", None, None),
        P("rep", "attn"),
        P("attn", "ffn"),
        P("rep", "ffn", "attn"),
        P("attn"),
        P("rep", "ffn", None),
        P("rep", "ffn", None),
        P("ffn", "attn", "rep"),
        P("ffn", "attn", "rep"),
        P("ffn", "attn", "rep"),
    )
    out_specs = P("rep", "ffn", "attn")
    return jax.shard_map(
        per_device, mesh=mesh, in_specs=in_specs, out_specs=out_specs, check_vma=False
    )
```

```python
import functools

import jax
import jax.numpy as jnp
from jax import lax
from jax.experimental import pallas as pl
from jax.experimental.pallas import tpu as pltpu
from jax.sharding import PartitionSpec as P

MESH = pl.DeviceIdType.MESH
BF = jnp.bfloat16
F32 = jnp.float32
NT = (((1,), (1,)), ((), ()))
NN = (((1,), (0,)), ((), ()))

CHIPS = 16
SIDE = 4
W = 224
WP = 256
CAP = 14
SLOT = 16
ROWS = 32
EFF = 640
HD = 256
KH = 2048
D = 7168

PLANE = sorted(
    ((df, dr, dc) for df in range(4) for dr in range(4) for dc in range(2) if df or dr or dc),
    key=lambda o: (-(min(o[0], 4 - o[0]) + min(o[1], 4 - o[1])), o),
)
XCORE = sorted(
    ((df, dc) for df in range(4) for dc in range(2) if df or dc),
    key=lambda o: (-min(o[0], 4 - o[0]), o),
)

RELAY = {0: (5, 1), 1: (4, 3, 2), 5: (8, 7, 6)}


def mm(a, b, dims=NN):
    return lax.dot_general(a, b, dims, preferred_element_type=F32)


def kernel(
    q_h, k_h, v_h, len_h, wo_h, res_h, gain_h, ids_h, gw_h, wg_h, wu_h, wd_h,
    out_ref,
    qv, kv, vv, lenv, resv, gainv, idsv, gwv, wo, wg, wu, wd,
    qs, att, xs, xr, ag1, us, rb, pad32, pad1, tok, xb, pb, r1, ra, s2, r2, ag2, eb, rr,
    ld, ss, rs, stay_s, back_s,
):
    a = lax.axis_index("attn")
    f = lax.axis_index("ffn")
    r = lax.axis_index("rep")
    c = lax.rem(a, 2)
    z = lax.div(a, 2)
    sg = 1 - 2 * c

    def zdev(d):
        return {"attn": lax.rem(z + d + CHIPS, CHIPS) * 2 + c}

    def zidx(d):
        return lax.rem(z + d + 2 * CHIPS, CHIPS)

    def pdev(o):
        df, dr, dc = o
        return {
            "attn": z * 2 + lax.rem(c + dc, 2),
            "ffn": lax.rem(f + df, 4),
            "rep": lax.rem(r + dr, 4),
        }

    sib = {"attn": z * 2 + 1 - c}

    loads = []

    def load(src, dst):
        cp = pltpu.make_async_copy(src, dst, ld.at[len(loads)])
        cp.start()
        loads.append(cp)
        return cp

    sent = []

    def send(src, dst, dev, arrival=None):
        k = len(sent)
        cp = pltpu.make_async_remote_copy(
            src_ref=src, dst_ref=dst, send_sem=ss.at[k],
            recv_sem=rs.at[k] if arrival is None else arrival,
            device_id=dev, device_id_type=MESH,
        )
        cp.start()
        sent.append(cp)
        return cp

    l_q = load(q_h.at[0], qv)
    l_k = load(k_h.at[0], kv)
    l_v = load(v_h.at[0], vv)
    l_len = load(len_h, lenv)

    barrier = pltpu.get_barrier_semaphore()
    peers = [zdev(d) for d in (5, -5)] + [pdev(o) for o in PLANE]
    peers += [zdev(d) for d in (3, -3, 2, -2, 1, -1)]
    for dev in peers:
        pl.semaphore_signal(barrier, inc=1, device_id=dev, device_id_type=MESH)

    l_ids = load(ids_h, idsv)
    l_gw = load(gw_h, gwv)
    l_res = load(res_h.at[0], resv)
    l_gain = load(gain_h, gainv)
    half = pl.multiple_of(c * KH, KH)
    other = pl.multiple_of((1 - c) * KH, KH)
    l_wo = load(wo_h.at[:, pl.ds(half, KH)], wo.at[c, pl.ds(0, W)])
    l_wg = load(wg_h.at[c], wg.at[c, pl.ds(0, W)])
    l_wu = load(wu_h.at[c], wu.at[c, pl.ds(0, W)])
    l_wd = load(wd_h.at[c], wd.at[c, pl.ds(0, W)])

    l_q.wait()
    q32 = qv[...].astype(F32)
    for i in range(4):
        for h in range(16):
            qs[i * 16 + h : i * 16 + h + 1, :] = q32[i : i + 1, h * HD : (h + 1) * HD]
    l_k.wait()
    l_len.wait()
    l_v.wait()
    position = lax.broadcasted_iota(jnp.int32, (16, HD), 1)
    for i in range(4):
        s = mm(qs[i * 16 : (i + 1) * 16, :].astype(BF), kv[i], NT) * (HD**-0.5)
        s = jnp.where(position < lenv[0:1, i : i + 1], s, F32(-1e30))
        e = jnp.exp(s - jnp.max(s, axis=1, keepdims=True))
        p = (e / jnp.sum(e, axis=1, keepdims=True)).astype(BF)
        o = mm(p, vv[i])
        for h in range(16):
            hh, hg, j = h // 8, (h % 8) // 4, h % 4
            for k in range(2):
                row = hg * 8 + k * 4 + i
                att[hh, row : row + 1, j * HD : (j + 1) * HD] = o[h : h + 1, :]
    rowi = lax.broadcasted_iota(jnp.int32, (16, 1024), 0)
    mine = lax.rem(lax.div(rowi, 4), 2) == c
    xs[...] = jnp.where(mine, att[1 - c], 0.0).astype(BF)

    pl.semaphore_wait(barrier, len(peers))
    x_cp = send(xs, xr, sib)
    x_wo = send(wo_h.at[:, pl.ds(other, KH)], wo.at[c, pl.ds(0, W)], sib)
    x_wg = send(wg_h.at[1 - c], wg.at[c, pl.ds(0, W)], sib)
    x_wu = send(wu_h.at[1 - c], wu.at[c, pl.ds(0, W)], sib)
    x_wd = send(wd_h.at[1 - c], wd.at[c, pl.ds(0, W)], sib)

    def gather_z(buf, arrived=None):
        got = {}

        def pass_on(o):
            block = buf.at[zidx(-o)]
            for to in RELAY[abs(o)]:
                if o == 0:
                    got[to] = send(block, block, zdev(to))
                    got[-to] = send(block, block, zdev(-to))
                elif to < 8:
                    sgn = 1 if o > 0 else -1
                    got[sgn * to] = send(block, block, zdev(sgn * to - o))

        pass_on(0)
        yield
        for o in (1, 5):
            for sgn in (1, -1):
                got[sgn * o].wait_recv()
                if o == 5 and sgn == -1:
                    far = buf.at[zidx(-5 * sg)]
                    got[8] = send(far, far, zdev(3 * sg))
                    pass_on(5)
                if o == 1 or sgn == -1:
                    pass_on(sgn * o)
            if o == 1 and arrived is not None:
                arrived((0, 1, -1))
        rest = [2, -2, 3, -3, 4, -4]
        for o in rest:
            got[o].wait_recv()
        if arrived is not None:
            arrived([5, -5] + rest)
        last = [6, -6, 7, -7, 8]
        for o in last:
            got[o].wait_recv()
        if arrived is not None:
            arrived(last)

    x_cp.wait_recv()
    ag1[z] = jnp.where(mine, att[c], 0.0).astype(BF) + xr[...]
    heads = gather_z(ag1)
    next(heads)

    for buf in (wo, wg, wu, wd):
        buf[:, W:WP, :] = jnp.zeros((2, WP - W, buf.shape[2]), BF)
    l_res.wait()
    l_gain.wait()
    l_ids.wait()
    l_gw.wait()
    pad32[...] = jnp.zeros((ROWS, WP), F32)
    pad32[:, 0:W] = resv[...].astype(F32)
    pad1[...] = jnp.zeros((1, WP), F32)
    pad1[:, 0:W] = gainv[...]
    spot = lax.broadcasted_iota(jnp.int32, (128, ROWS), 0)
    hits = jnp.zeros((128, ROWS), F32)
    share = jnp.zeros((128, ROWS), F32)
    for k in range(3):
        same = idsv[k] == lax.div(spot, SLOT)
        hits = hits + jnp.where(same, 1.0, 0.0)
        share = share + jnp.where(same, gwv[k], 0.0)
    earlier = lax.broadcasted_iota(jnp.int32, (ROWS, ROWS), 0) < lax.broadcasted_iota(
        jnp.int32, (ROWS, ROWS), 1
    )
    before = mm(hits.astype(BF), jnp.where(earlier, 1.0, 0.0).astype(BF))
    placed = before == lax.rem(spot, SLOT).astype(F32)
    pick = jnp.where(placed, hits, 0.0).astype(BF)
    share = jnp.where(placed, share, 0.0)
    eye = lax.broadcasted_iota(jnp.int32, (ROWS, ROWS), 0) == lax.broadcasted_iota(
        jnp.int32, (ROWS, ROWS), 1
    )
    eye = jnp.where(eye, 1.0, 0.0).astype(BF)
    share_hi = share.astype(BF)
    share_lo = (share - share_hi.astype(F32)).astype(BF)
    share_hi = jnp.concatenate([mm(eye, share_hi, NT).astype(BF)] * 4, axis=1)
    share_lo = jnp.concatenate([mm(eye, share_lo, NT).astype(BF)] * 4, axis=1)


    for _ in heads:
        pass
    l_wo.wait()
    x_wo.wait_recv()

    rows = ag1[...].reshape(CHIPS * 16, 1024)
    for s in range(2):
        p0 = mm(rows, wo[s, :, 0:1024], NT).reshape(CHIPS, 16, WP)
        p1 = mm(rows, wo[s, :, 1024:2048], NT).reshape(CHIPS, 16, WP)
        u = p0[:, 0:8] + p1[:, 8:16]
        us[s] = u.reshape(4, ROWS, WP).astype(BF)
    pending = []
    for df, dc in XCORE:
        q = lax.rem(f + df, 4)
        s = lax.rem(c + dc, 2)
        pending.append(send(us.at[s, q], rb.at[f * 2 + c], pdev((df, 0, dc))))
    rb[f * 2 + c] = us[c, f]
    hidden = pad32[...]
    for cp in pending:
        cp.wait_recv()
    for k in range(8):
        hidden = hidden + rb[k].astype(F32)
    hid = hidden.astype(BF).astype(F32)
    squares = jnp.sum(hid * hid, axis=1, keepdims=True)
    sq_hi = squares.astype(BF).astype(F32)
    lane2 = lax.broadcasted_iota(jnp.int32, (ROWS, WP), 1)
    normed = jnp.where(
        lane2 == W, sq_hi, jnp.where(lane2 == W + 1, squares - sq_hi, hid * pad1[...])
    ).astype(BF)
    tok[...] = mm(pick, normed).astype(BF).reshape(8, SLOT, WP)

    pending = []
    for o in PLANE:
        e = lax.rem(f + o[0], 4) * 2 + lax.rem(c + o[2], 2)
        pending.append(send(tok.at[e], xb.at[c, r * 4 + f], pdev(o)))
    xb[c, r * 4 + f] = tok[f * 2 + c]
    l_wg.wait()
    x_wg.wait_recv()
    l_wu.wait()
    x_wu.wait_recv()
    for cp in pending:
        cp.wait_recv()
    x0 = xb[0].reshape(256, WP)
    x1 = xb[1].reshape(256, WP)
    ones = lax.broadcasted_iota(jnp.int32, (16, WP), 1)
    ones = jnp.where((ones == W) | (ones == W + 1), 1.0, 0.0).astype(BF)
    sq = (mm(ones, x0, NT) + mm(ones, x1, NT))[0:1, :]
    sq_hi = sq.astype(BF).astype(F32)
    sq_lo = sq - sq_hi
    gate = mm(x0, wg[0]) + mm(x1, wg[1])
    slot = lax.rem(lax.broadcasted_iota(jnp.int32, (256, 256), 0), SLOT)
    head = jnp.where(slot == CAP, sq_hi, jnp.where(slot == CAP + 1, sq_lo, gate[:, 0:256]))
    pb[:, :, 0:256] = head.astype(BF).reshape(CHIPS, SLOT, 256)
    pb[:, :, 256:EFF] = gate[:, 256:EFF].astype(BF).reshape(CHIPS, SLOT, EFF - 256)
    up = mm(x0, wu[0]) + mm(x1, wu[1])
    pb[:, :, EFF : 2 * EFF] = up.astype(BF).reshape(CHIPS, SLOT, EFF)

    sides = ((0, 1), (1, -1))
    leaf = {}
    for side, sgn in sides:
        leaf[side, 7] = send(pb.at[zidx(-sgn * 7)], r1.at[side, 0], zdev(-sgn))
    anti = send(pb.at[zidx(8)], ra, zdev(-3 * sg))
    for k, o in ((2, 4), (3, 2)):
        for side, sgn in sides:
            leaf[side, o] = send(pb.at[zidx(-sgn * o)], r1.at[side, k], zdev(-sgn))
    pending = []
    for side, sgn in sides:
        leaf[side, 7].wait_recv()
        acc = pb[zidx(-sgn * 6)].astype(F32) + r1[side, 0].astype(F32)
        s2[side, 0] = acc.astype(BF)
        leaf[side, 6] = send(s2.at[side, 0], r1.at[side, 1], zdev(-sgn))
    for side, sgn in sides:
        leaf[side, 4].wait_recv()
        acc = pb[zidx(-sgn * 3)].astype(F32) + r1[side, 2].astype(F32)
        s2[side, 1] = acc.astype(BF)
        pending.append(send(s2.at[side, 1], r2.at[side, 1], zdev(-sgn * 3)))
    anti.wait_recv()
    for side, sgn in sides:
        leaf[side, 6].wait_recv()
        acc = pb[zidx(-sgn * 5)].astype(F32) + r1[side, 1].astype(F32)
        acc = acc + jnp.where(c == side, ra[...].astype(F32), 0.0)
        s2[side, 2] = acc.astype(BF)
        pending.append(send(s2.at[side, 2], r2.at[side, 0], zdev(-sgn * 5)))
    for side, sgn in sides:
        leaf[side, 2].wait_recv()
        acc = pb[zidx(-sgn)].astype(F32) + r1[side, 3].astype(F32)
        s2[side, 3] = acc.astype(BF)
        pending.append(send(s2.at[side, 3], r2.at[side, 2], zdev(-sgn)))
    total = pb[z].astype(F32)
    for cp in pending:
        cp.wait_recv()
    for side in range(2):
        for k in range(3):
            total = total + r2[side, k].astype(F32)
    sq = total[CAP : CAP + 1, 0:256] + total[CAP + 1 : CAP + 2, 0:256]
    row = lax.broadcasted_iota(jnp.int32, (SLOT, 256), 0)
    lane3 = lax.broadcasted_iota(jnp.int32, (SLOT, 256), 1)
    sq = jnp.sum(jnp.where(lane3 == z * SLOT + row, sq, 0.0), axis=1, keepdims=True)
    rinv = lax.rsqrt(sq / D + 1e-6)
    gate = total[:, 0:EFF] * rinv
    up = total[:, EFF : 2 * EFF] * rinv
    act = gate / (1.0 + jnp.exp(-gate)) * up
    live = lax.broadcasted_iota(jnp.int32, (SLOT, EFF), 0) < CAP
    ag2[z] = jnp.where(live, act, 0.0).astype(BF)

    l_wd.wait()
    x_wd.wait_recv()
    me = r * 8 + f * 2 + c
    stay = []

    def give_back(offsets):
        first = len(stay)
        rows = jnp.concatenate([ag2[zidx(-o)] for o in offsets], axis=0)
        for s in range(2):
            out = mm(rows, wd[s], NT).astype(BF).reshape(len(offsets), SLOT, WP)
            eb[s, first : first + len(offsets)] = out
        for k, o in enumerate(offsets):
            b = zidx(-o)
            fo, ro = lax.rem(b, 4), lax.div(b, 4)
            i = first + k
            send(eb.at[1 - c, i], rr.at[me], {"attn": z * 2 + 1 - c, "ffn": fo, "rep": ro}, back_s.at[me])
            cp = pltpu.make_async_remote_copy(
                src_ref=eb.at[c, i], dst_ref=rr.at[me], send_sem=stay_s.at[i],
                recv_sem=back_s.at[me], device_id={"ffn": fo, "rep": ro}, device_id_type=MESH,
            )
            away = b != r * 4 + f
            stay.append((away, cp))

            @pl.when(away)
            def _():
                cp.start()

            @pl.when(jnp.logical_not(away))
            def _():
                rr[me] = eb[c, i]

    for _ in gather_z(ag2, give_back):
        pass
    for j in range(1, 32):
        k = lax.rem(me + j, 32)
        pltpu.make_async_remote_copy(
            src_ref=eb.at[0, 0], dst_ref=rr.at[k], send_sem=stay_s.at[0],
            recv_sem=back_s.at[k], device_id=sib, device_id_type=MESH,
        ).wait_recv()
    back = rr[...].reshape(512, WP)
    mixed = hidden + mm(share_hi, back) + mm(share_lo, back)
    out_ref[0] = mixed[:, 0:W]
    for cp in sent:
        cp.wait_send()
    for away, cp in stay:
        @pl.when(away)
        def _():
            cp.wait_send()


N_SENT = 5 + 15 + 7 + 31 + 15 + 15 + 16


def per_device(q, k, v, lens, wo, res, gain, ids, gw, wg, wu, wd):
    ids = jnp.transpose(ids, (2, 0, 1))
    gw = jnp.transpose(gw, (2, 0, 1))
    any_spec = pl.BlockSpec(memory_space=pl.ANY)
    vm = pltpu.VMEM
    dma = pltpu.SemaphoreType.DMA
    return pl.pallas_call(
        kernel,
        name="layer",
        out_shape=pltpu.VMEM((1, ROWS, W), F32),
        in_specs=[any_spec] * 12,
        out_specs=pl.BlockSpec(memory_space=pltpu.VMEM),
        scratch_shapes=[
            vm((4, 4096), BF),
            vm((4, 256, HD), BF),
            vm((4, 256, HD), BF),
            vm((1, 4), jnp.int32),
            vm((ROWS, W), BF),
            vm((1, W), F32),
            vm((3, 1, ROWS), jnp.int32),
            vm((3, 1, ROWS), F32),
            vm((2, WP, KH), BF),
            vm((2, WP, EFF), BF),
            vm((2, WP, EFF), BF),
            vm((2, WP, EFF), BF),
            vm((64, HD), F32),
            vm((2, 16, 1024), F32),
            vm((16, 1024), BF),
            vm((16, 1024), BF),
            vm((CHIPS, 16, 1024), BF),
            vm((2, 4, ROWS, WP), BF),
            vm((8, ROWS, WP), BF),
            vm((ROWS, WP), F32),
            vm((1, WP), F32),
            vm((8, SLOT, WP), BF),
            vm((2, 16, SLOT, WP), BF),
            vm((CHIPS, SLOT, 2 * EFF), BF),
            vm((2, 4, SLOT, 2 * EFF), BF),
            vm((SLOT, 2 * EFF), BF),
            vm((2, 4, SLOT, 2 * EFF), BF),
            vm((2, 3, SLOT, 2 * EFF), BF),
            vm((CHIPS, SLOT, EFF), BF),
            vm((2, 16, SLOT, WP), BF),
            vm((32, SLOT, WP), BF),
            dma((12,)),
            dma((N_SENT,)),
            dma((N_SENT,)),
            dma((16,)),
            dma((32,)),
        ],
        compiler_params=pltpu.CompilerParams(
            collective_id=0, has_side_effects=True, vmem_limit_bytes=56 * 1024 * 1024
        ),
    )(q, k, v, lens, wo, res, gain.reshape(1, W), ids, gw, wg, wu, wd)


def solution(mesh):
    in_specs = (
        P("rep", "attn", "ffn"),
        P("rep", "attn", None, None),
        P("rep", "attn", None, None),
        P("rep", "attn"),
        P("attn", "ffn"),
        P("rep", "ffn", "attn"),
        P("attn"),
        P("rep", "ffn", None),
        P("rep", "ffn", None),
        P("ffn", "attn", "rep"),
        P("ffn", "attn", "rep"),
        P("ffn", "attn", "rep"),
    )
    out_specs = P("rep", "ffn", "attn")
    return jax.shard_map(
        per_device, mesh=mesh, in_specs=in_specs, out_specs=out_specs, check_vma=False
    )
```

```python
import functools

import jax
import jax.numpy as jnp
from jax import lax
from jax.experimental import pallas as pl
from jax.experimental.pallas import tpu as pltpu
from jax.sharding import PartitionSpec as P

MESH = pl.DeviceIdType.MESH
BF = jnp.bfloat16
F32 = jnp.float32
NT = (((1,), (1,)), ((), ()))
NN = (((1,), (0,)), ((), ()))

CHIPS = 16
SIDE = 4
W = 224
WP = 256
CAP = 14
SLOT = 16
ROWS = 32
EFF = 640
EA, EB = 384, 256
TAIL = 512
HD = 256
KH = 2048
D = 7168

PLANE = sorted(
    ((df, dr, dc) for df in range(4) for dr in range(4) for dc in range(2) if df or dr or dc),
    key=lambda o: (-(min(o[0], 4 - o[0]) + min(o[1], 4 - o[1])), o),
)
XCORE = sorted(
    ((df, dc) for df in range(4) for dc in range(2) if df or dc),
    key=lambda o: (-min(o[0], 4 - o[0]), o),
)

FIRST = (0, 1, -1)
MIDDLE = (5, -5, 2, -2, 3, -3, 4, -4)
LAST = (6, -6, 7, -7, 8)
RELAY = {0: (5, 1), 1: (4, 3, 2), 5: (8, 7, 6)}


def mm(a, b, dims=NN):
    return lax.dot_general(a, b, dims, preferred_element_type=F32)


def kernel(
    q_h, k_h, v_h, len_h, wo_h, res_h, gain_h, ids_h, gw_h, wg_h, wu_h, wd_h,
    out_ref,
    qv, kv, vv, lenv, resv, gainv, idsv, gwv, wo, wg, wu, wd,
    qs, att, xs, xr, ag1, us, rb, pad32, pad1, tok, xb, pb_a, r1_a, ra_a, s2_a, r2_a, pb_b, r1_b, ra_b, s2_b, r2_b, last_up, ag2_a, ag2_b, eb, rr,
    ld, ss, rs, stay_s, back_s,
):
    a = lax.axis_index("attn")
    f = lax.axis_index("ffn")
    r = lax.axis_index("rep")
    c = lax.rem(a, 2)
    z = lax.div(a, 2)
    sg = 1 - 2 * c

    def zdev(d):
        return {"attn": lax.rem(z + d + CHIPS, CHIPS) * 2 + c}

    def zidx(d):
        return lax.rem(z + d + 2 * CHIPS, CHIPS)

    def pdev(o):
        df, dr, dc = o
        return {
            "attn": z * 2 + lax.rem(c + dc, 2),
            "ffn": lax.rem(f + df, 4),
            "rep": lax.rem(r + dr, 4),
        }

    sib = {"attn": z * 2 + 1 - c}

    loads = []

    def load(src, dst):
        cp = pltpu.make_async_copy(src, dst, ld.at[len(loads)])
        cp.start()
        loads.append(cp)
        return cp

    sent = []

    def send(src, dst, dev, arrival=None):
        k = len(sent)
        cp = pltpu.make_async_remote_copy(
            src_ref=src, dst_ref=dst, send_sem=ss.at[k],
            recv_sem=rs.at[k] if arrival is None else arrival,
            device_id=dev, device_id_type=MESH,
        )
        cp.start()
        sent.append(cp)
        return cp

    l_q = load(q_h.at[0], qv)
    l_k = load(k_h.at[0], kv)
    l_v = load(v_h.at[0], vv)
    l_len = load(len_h, lenv)

    barrier = pltpu.get_barrier_semaphore()
    peers = [zdev(d) for d in (5, -5)] + [pdev(o) for o in PLANE]
    peers += [zdev(d) for d in (3, -3, 2, -2, 1, -1)]
    for dev in peers:
        pl.semaphore_signal(barrier, inc=1, device_id=dev, device_id_type=MESH)

    l_ids = load(ids_h, idsv)
    l_gw = load(gw_h, gwv)
    l_res = load(res_h.at[0], resv)
    l_gain = load(gain_h, gainv)
    half = pl.multiple_of(c * KH, KH)
    other = pl.multiple_of((1 - c) * KH, KH)
    l_wo = load(wo_h.at[:, pl.ds(half, KH)], wo.at[c, pl.ds(0, W)])
    l_wg = load(wg_h.at[c], wg.at[c, pl.ds(0, W)])
    l_wu = load(wu_h.at[c], wu.at[c, pl.ds(0, W)])
    l_wd = load(wd_h.at[c], wd.at[c, pl.ds(0, W)])

    l_q.wait()
    q32 = qv[...].astype(F32)
    for i in range(4):
        for h in range(16):
            qs[i * 16 + h : i * 16 + h + 1, :] = q32[i : i + 1, h * HD : (h + 1) * HD]
    l_k.wait()
    l_len.wait()
    l_v.wait()
    position = lax.broadcasted_iota(jnp.int32, (16, HD), 1)
    for i in range(4):
        s = mm(qs[i * 16 : (i + 1) * 16, :].astype(BF), kv[i], NT) * (HD**-0.5)
        s = jnp.where(position < lenv[0:1, i : i + 1], s, F32(-1e30))
        e = jnp.exp(s - jnp.max(s, axis=1, keepdims=True))
        p = (e / jnp.sum(e, axis=1, keepdims=True)).astype(BF)
        o = mm(p, vv[i])
        for h in range(16):
            hh, hg, j = h // 8, (h % 8) // 4, h % 4
            for k in range(2):
                row = hg * 8 + k * 4 + i
                att[hh, row : row + 1, j * HD : (j + 1) * HD] = o[h : h + 1, :]
    rowi = lax.broadcasted_iota(jnp.int32, (16, 1024), 0)
    mine = lax.rem(lax.div(rowi, 4), 2) == c
    xs[...] = jnp.where(mine, att[1 - c], 0.0).astype(BF)

    pl.semaphore_wait(barrier, len(peers))
    x_cp = send(xs, xr, sib)
    x_wo = send(wo_h.at[:, pl.ds(other, KH)], wo.at[c, pl.ds(0, W)], sib)
    x_wg = send(wg_h.at[1 - c], wg.at[c, pl.ds(0, W)], sib)
    x_wu = send(wu_h.at[1 - c], wu.at[c, pl.ds(0, W)], sib)
    x_wd = send(wd_h.at[1 - c], wd.at[c, pl.ds(0, W)], sib)

    def gather_z(buf):
        got = {}

        def pass_on(o):
            block = buf.at[zidx(-o)]
            for to in RELAY[abs(o)]:
                if o == 0:
                    got[to] = send(block, block, zdev(to))
                    got[-to] = send(block, block, zdev(-to))
                elif to < 8:
                    sgn = 1 if o > 0 else -1
                    got[sgn * to] = send(block, block, zdev(sgn * to - o))

        pass_on(0)
        yield
        for sgn in (1, -1):
            got[sgn].wait_recv()
            pass_on(sgn)
        yield
        got[5].wait_recv()
        got[-5].wait_recv()
        far = buf.at[zidx(-5 * sg)]
        got[8] = send(far, far, zdev(3 * sg))
        pass_on(5)
        pass_on(-5)
        yield
        for o in MIDDLE[2:]:
            got[o].wait_recv()
        yield
        for o in LAST:
            got[o].wait_recv()

    x_cp.wait_recv()
    ag1[z] = jnp.where(mine, att[c], 0.0).astype(BF) + xr[...]
    heads = gather_z(ag1)
    next(heads)

    for buf in (wo, wg, wu, wd):
        buf[:, W:WP, :] = jnp.zeros((2, WP - W, buf.shape[2]), BF)
    l_res.wait()
    l_gain.wait()
    l_ids.wait()
    l_gw.wait()
    pad32[...] = jnp.zeros((ROWS, WP), F32)
    pad32[:, 0:W] = resv[...].astype(F32)
    pad1[...] = jnp.zeros((1, WP), F32)
    pad1[:, 0:W] = gainv[...]
    spot = lax.broadcasted_iota(jnp.int32, (128, ROWS), 0)
    hits = jnp.zeros((128, ROWS), F32)
    share = jnp.zeros((128, ROWS), F32)
    for k in range(3):
        same = idsv[k] == lax.div(spot, SLOT)
        hits = hits + jnp.where(same, 1.0, 0.0)
        share = share + jnp.where(same, gwv[k], 0.0)
    earlier = lax.broadcasted_iota(jnp.int32, (ROWS, ROWS), 0) < lax.broadcasted_iota(
        jnp.int32, (ROWS, ROWS), 1
    )
    before = mm(hits.astype(BF), jnp.where(earlier, 1.0, 0.0).astype(BF))
    placed = before == lax.rem(spot, SLOT).astype(F32)
    pick = jnp.where(placed, hits, 0.0).astype(BF)
    share = jnp.where(placed, share, 0.0)
    eye = lax.broadcasted_iota(jnp.int32, (ROWS, ROWS), 0) == lax.broadcasted_iota(
        jnp.int32, (ROWS, ROWS), 1
    )
    eye = jnp.where(eye, 1.0, 0.0).astype(BF)
    share_hi = share.astype(BF)
    share_lo = (share - share_hi.astype(F32)).astype(BF)
    share_hi = jnp.concatenate([mm(eye, share_hi, NT).astype(BF)] * 4, axis=1)
    share_lo = jnp.concatenate([mm(eye, share_lo, NT).astype(BF)] * 4, axis=1)


    for _ in heads:
        pass
    l_wo.wait()
    x_wo.wait_recv()

    rows = ag1[...].reshape(CHIPS * 16, 1024)
    for s in range(2):
        p0 = mm(rows, wo[s, :, 0:1024], NT).reshape(CHIPS, 16, WP)
        p1 = mm(rows, wo[s, :, 1024:2048], NT).reshape(CHIPS, 16, WP)
        u = p0[:, 0:8] + p1[:, 8:16]
        us[s] = u.reshape(4, ROWS, WP).astype(BF)
    pending = []
    for df, dc in XCORE:
        q = lax.rem(f + df, 4)
        s = lax.rem(c + dc, 2)
        pending.append(send(us.at[s, q], rb.at[f * 2 + c], pdev((df, 0, dc))))
    rb[f * 2 + c] = us[c, f]
    hidden = pad32[...]
    for cp in pending:
        cp.wait_recv()
    for k in range(8):
        hidden = hidden + rb[k].astype(F32)
    hid = hidden.astype(BF).astype(F32)
    squares = jnp.sum(hid * hid, axis=1, keepdims=True)
    sq_hi = squares.astype(BF).astype(F32)
    lane2 = lax.broadcasted_iota(jnp.int32, (ROWS, WP), 1)
    normed = jnp.where(
        lane2 == W, sq_hi, jnp.where(lane2 == W + 1, squares - sq_hi, hid * pad1[...])
    ).astype(BF)
    tok[...] = mm(pick, normed).astype(BF).reshape(8, SLOT, WP)

    pending = []
    for o in PLANE:
        e = lax.rem(f + o[0], 4) * 2 + lax.rem(c + o[2], 2)
        pending.append(send(tok.at[e], xb.at[c, r * 4 + f], pdev(o)))
    xb[c, r * 4 + f] = tok[f * 2 + c]
    l_wg.wait()
    x_wg.wait_recv()
    l_wu.wait()
    x_wu.wait_recv()
    for cp in pending:
        cp.wait_recv()
    x0 = xb[0].reshape(256, WP)
    x1 = xb[1].reshape(256, WP)
    ones = lax.broadcasted_iota(jnp.int32, (16, WP), 1)
    ones = jnp.where((ones == W) | (ones == W + 1), 1.0, 0.0).astype(BF)
    sq = (mm(ones, x0, NT) + mm(ones, x1, NT))[0:1, :]
    sq_hi = sq.astype(BF).astype(F32)
    sq_lo = sq - sq_hi
    def project(w, lo, hi):
        out = mm(x0, w[0, :, lo:hi]) + mm(x1, w[1, :, lo:hi])
        return out.reshape(CHIPS, SLOT, hi - lo)

    tail = project(wu, TAIL, EFF)
    slot = lax.broadcasted_iota(jnp.int32, (CHIPS, SLOT, 128), 1)

    def put(buf, column, base, first_tile):
        for j in range(base.shape[2] // 128):
            t = first_tile + j
            if t in (2, 3):
                low = sq_hi[:, (t - 2) * 128 : (t - 1) * 128].reshape(1, 1, 128)
            elif t in (4, 5):
                low = sq_lo[:, (t - 4) * 128 : (t - 3) * 128].reshape(1, 1, 128)
            else:
                k = 9 + t if t < 2 else 5 + t
                low = tail[:, k : k + 1, :]
            piece = jnp.where(slot == CAP + 1, low, base[:, :, j * 128 : (j + 1) * 128])
            piece = jnp.where(slot == CAP, tail[:, t : t + 1, :], piece)
            buf[:, :, column + j * 128 : column + (j + 1) * 128] = piece.astype(BF)

    sides = ((0, 1), (1, -1))

    class Sum:
        def __init__(self, pb, r1, ra, s2, r2):
            self.pb, self.r1, self.ra, self.s2, self.r2 = pb, r1, ra, s2, r2
            self.leaf, self.ends = {}, []

        def leaves(self):
            for k, (o, d) in enumerate(((7, -1), (5, 1), (4, -2), (3, -1), (1, 1))):
                for side, sgn in sides:
                    src = self.pb.at[zidx(-sgn * o)]
                    self.leaf[side, k] = send(src, self.r1.at[side, k], zdev(sgn * d))
                if o == 5:
                    self.anti = send(self.pb.at[zidx(8)], self.ra, zdev(-2 * sg))

        def relay(self, slot, o, parts):
            for side, sgn in sides:
                acc = self.pb[zidx(-sgn * o)].astype(F32)
                for k in parts:
                    self.leaf[side, k].wait_recv()
                    acc = acc + self.r1[side, k].astype(F32)
                if o == 6:
                    if side == 0:
                        self.anti.wait_recv()
                    acc = acc + jnp.where(c == side, self.ra[...].astype(F32), 0.0)
                self.s2[side, slot] = acc.astype(BF)
                src = self.s2.at[side, slot]
                self.ends.append(send(src, self.r2.at[side, slot], zdev(-sgn * o)))

        def total(self):
            out = self.pb[z].astype(F32)
            for cp in self.ends:
                cp.wait_recv()
            for side in range(2):
                for k in range(2):
                    out = out + self.r2[side, k].astype(F32)
            return out

    sum_a, sum_b = Sum(pb_a, r1_a, ra_a, s2_a, r2_a), Sum(pb_b, r1_b, ra_b, s2_b, r2_b)
    put(pb_a, 0, project(wg, 0, EA), 0)
    put(pb_a, EA, project(wu, 0, EA), 3)
    sum_a.leaves()
    put(pb_b, 0, project(wg, EA, EFF), 6)
    put(pb_b, EB, project(wu, EA, TAIL), 8)
    sum_b.leaves()
    sum_a.relay(0, 6, (0, 1))
    sum_b.relay(0, 6, (0, 1))
    sum_a.relay(1, 2, (2, 3, 4))
    sum_b.relay(1, 2, (2, 3, 4))

    def activate(gate, up):
        gate, up = gate * rinv, up * rinv
        act = gate / (1.0 + jnp.exp(-gate)) * up
        live = lax.broadcasted_iota(jnp.int32, act.shape, 0) < CAP
        return jnp.where(live, act, 0.0).astype(BF)

    total = sum_a.total()
    for t in range(6):
        last_up[t : t + 1, :] = total[CAP : CAP + 1, t * 128 : (t + 1) * 128]
    for t in range(2):
        last_up[9 + t : 10 + t, :] = total[CAP + 1 : CAP + 2, t * 128 : (t + 1) * 128]
    sq = total[CAP + 1 : CAP + 2, 256:512] + total[CAP + 1 : CAP + 2, 512:768]
    row = lax.broadcasted_iota(jnp.int32, (SLOT, 256), 0)
    lane3 = lax.broadcasted_iota(jnp.int32, (SLOT, 256), 1)
    sq = jnp.sum(jnp.where(lane3 == z * SLOT + row, sq, 0.0), axis=1, keepdims=True)
    rinv = lax.rsqrt(sq / D + 1e-6)
    ag2_a[z] = activate(total[:, 0:EA], total[:, EA : 2 * EA])
    rows_a = gather_z(ag2_a)
    next(rows_a)
    total = sum_b.total()
    for t in range(3):
        last_up[6 + t : 7 + t, :] = total[CAP : CAP + 1, t * 128 : (t + 1) * 128]
        last_up[11 + t : 12 + t, :] = total[CAP + 1 : CAP + 2, t * 128 : (t + 1) * 128]
    last_up[CAP:SLOT, :] = jnp.zeros((SLOT - CAP, 128), F32)
    up = jnp.concatenate([total[:, EB : EB + 128], last_up[...]], axis=1)
    ag2_b[z] = activate(total[:, 0:EB], up)
    rows_b = gather_z(ag2_b)
    next(rows_b)

    l_wd.wait()
    x_wd.wait_recv()
    me = r * 8 + f * 2 + c
    stay = []

    def give_back(offsets):
        first = len(stay)
        act_a = jnp.concatenate([ag2_a[zidx(-o)] for o in offsets], axis=0)
        act_b = jnp.concatenate([ag2_b[zidx(-o)] for o in offsets], axis=0)
        for s in range(2):
            out = mm(act_a, wd[s, :, 0:EA], NT) + mm(act_b, wd[s, :, EA:EFF], NT)
            eb[s, first : first + len(offsets)] = out.astype(BF).reshape(len(offsets), SLOT, WP)
        for k, o in enumerate(offsets):
            b = zidx(-o)
            fo, ro = lax.rem(b, 4), lax.div(b, 4)
            i = first + k
            send(eb.at[1 - c, i], rr.at[me], {"attn": z * 2 + 1 - c, "ffn": fo, "rep": ro}, back_s.at[me])
            cp = pltpu.make_async_remote_copy(
                src_ref=eb.at[c, i], dst_ref=rr.at[me], send_sem=stay_s.at[i],
                recv_sem=back_s.at[me], device_id={"ffn": fo, "rep": ro}, device_id_type=MESH,
            )
            away = b != r * 4 + f
            stay.append((away, cp))

            @pl.when(away)
            def _():
                cp.start()

            @pl.when(jnp.logical_not(away))
            def _():
                rr[me] = eb[c, i]

    next(rows_a)
    next(rows_b)
    next(rows_a)
    give_back(FIRST)
    next(rows_b)
    next(rows_a)
    next(rows_b)
    give_back(MIDDLE)
    for rows in (rows_a, rows_b):
        for _ in rows:
            pass
    give_back(LAST)
    for j in range(1, 32):
        k = lax.rem(me + j, 32)
        pltpu.make_async_remote_copy(
            src_ref=eb.at[0, 0], dst_ref=rr.at[k], send_sem=stay_s.at[0],
            recv_sem=back_s.at[k], device_id=sib, device_id_type=MESH,
        ).wait_recv()
    back = rr[...].reshape(512, WP)
    mixed = hidden + mm(share_hi, back) + mm(share_lo, back)
    out_ref[0] = mixed[:, 0:W]
    for cp in sent:
        cp.wait_send()
    for away, cp in stay:
        @pl.when(away)
        def _():
            cp.wait_send()


N_SENT = 5 + 15 + 7 + 31 + 30 + 30 + 16


def per_device(q, k, v, lens, wo, res, gain, ids, gw, wg, wu, wd):
    ids = jnp.transpose(ids, (2, 0, 1))
    gw = jnp.transpose(gw, (2, 0, 1))
    any_spec = pl.BlockSpec(memory_space=pl.ANY)
    vm = pltpu.VMEM
    dma = pltpu.SemaphoreType.DMA
    return pl.pallas_call(
        kernel,
        name="layer",
        out_shape=pltpu.VMEM((1, ROWS, W), F32),
        in_specs=[any_spec] * 12,
        out_specs=pl.BlockSpec(memory_space=pltpu.VMEM),
        scratch_shapes=[
            vm((4, 4096), BF),
            vm((4, 256, HD), BF),
            vm((4, 256, HD), BF),
            vm((1, 4), jnp.int32),
            vm((ROWS, W), BF),
            vm((1, W), F32),
            vm((3, 1, ROWS), jnp.int32),
            vm((3, 1, ROWS), F32),
            vm((2, WP, KH), BF),
            vm((2, WP, EFF), BF),
            vm((2, WP, EFF), BF),
            vm((2, WP, EFF), BF),
            vm((64, HD), F32),
            vm((2, 16, 1024), F32),
            vm((16, 1024), BF),
            vm((16, 1024), BF),
            vm((CHIPS, 16, 1024), BF),
            vm((2, 4, ROWS, WP), BF),
            vm((8, ROWS, WP), BF),
            vm((ROWS, WP), F32),
            vm((1, WP), F32),
            vm((8, SLOT, WP), BF),
            vm((2, 16, SLOT, WP), BF),
            vm((CHIPS, SLOT, 2 * EA), BF),
            vm((2, 5, SLOT, 2 * EA), BF),
            vm((SLOT, 2 * EA), BF),
            vm((2, 2, SLOT, 2 * EA), BF),
            vm((2, 2, SLOT, 2 * EA), BF),
            vm((CHIPS, SLOT, EB + 128), BF),
            vm((2, 5, SLOT, EB + 128), BF),
            vm((SLOT, EB + 128), BF),
            vm((2, 2, SLOT, EB + 128), BF),
            vm((2, 2, SLOT, EB + 128), BF),
            vm((SLOT, 128), F32),
            vm((CHIPS, SLOT, EA), BF),
            vm((CHIPS, SLOT, EB), BF),
            vm((2, 16, SLOT, WP), BF),
            vm((32, SLOT, WP), BF),
            dma((12,)),
            dma((N_SENT,)),
            dma((N_SENT,)),
            dma((16,)),
            dma((32,)),
        ],
        compiler_params=pltpu.CompilerParams(
            collective_id=0, has_side_effects=True, vmem_limit_bytes=56 * 1024 * 1024
        ),
    )(q, k, v, lens, wo, res, gain.reshape(1, W), ids, gw, wg, wu, wd)


def solution(mesh):
    in_specs = (
        P("rep", "attn", "ffn"),
        P("rep", "attn", None, None),
        P("rep", "attn", None, None),
        P("rep", "attn"),
        P("attn", "ffn"),
        P("rep", "ffn", "attn"),
        P("attn"),
        P("rep", "ffn", None),
        P("rep", "ffn", None),
        P("ffn", "attn", "rep"),
        P("ffn", "attn", "rep"),
        P("ffn", "attn", "rep"),
    )
    out_specs = P("rep", "ffn", "attn")
    return jax.shard_map(
        per_device, mesh=mesh, in_specs=in_specs, out_specs=out_specs, check_vma=False
    )
```

```python
import functools

import jax
import jax.numpy as jnp
from jax import lax
from jax.experimental import pallas as pl
from jax.experimental.pallas import tpu as pltpu
from jax.sharding import PartitionSpec as P

MESH = pl.DeviceIdType.MESH
BF = jnp.bfloat16
F32 = jnp.float32
NT = (((1,), (1,)), ((), ()))
NN = (((1,), (0,)), ((), ()))

CHIPS = 16
SIDE = 4
W = 224
WP = 256
CAP = 14
SLOT = 16
ROWS = 32
EFF = 640
EA, EB = 384, 256
TAIL = 512
HD = 256
KH = 2048
D = 7168

PLANE = sorted(
    ((df, dr, dc) for df in range(4) for dr in range(4) for dc in range(2) if df or dr or dc),
    key=lambda o: (-(min(o[0], 4 - o[0]) + min(o[1], 4 - o[1])), o),
)
XCORE = sorted(
    ((df, dc) for df in range(4) for dc in range(2) if df or dc),
    key=lambda o: (-min(o[0], 4 - o[0]), o),
)

FIRST = (0, 1, -1)
MIDDLE = (5, -5, 2, -2, 3, -3, 4, -4)
LAST = (6, -6, 7, -7, 8)
RELAY = {0: (5, 1), 1: (4, 3, 2), 5: (8, 7, 6)}


def mm(a, b, dims=NN):
    return lax.dot_general(a, b, dims, preferred_element_type=F32)


def kernel(
    q_h, k_h, v_h, len_h, wo_h, res_h, gain_h, ids_h, gw_h, wg_h, wu_h, wd_h,
    out_ref,
    qv, kv, vv, lenv, resv, gainv, idsv, gwv, wo, wg, wu, wd,
    qs, att, xs, xr, ag1, us, rb, pad32, pad1, tok, xb, pb_a, r1_a, s2_a, r2_a, pb_b, r1_b, s2_b, r2_b, last_up, ag2_a, ag2_b, eb, rr,
    ld, ss, rs, out_s, in_s,
):
    a = lax.axis_index("attn")
    f = lax.axis_index("ffn")
    r = lax.axis_index("rep")
    c = lax.rem(a, 2)
    z = lax.div(a, 2)
    sg = 1 - 2 * c

    def zdev(d):
        return {"attn": lax.rem(z + d + CHIPS, CHIPS) * 2 + c}

    def zidx(d):
        return lax.rem(z + d + 2 * CHIPS, CHIPS)

    def pdev(o):
        df, dr, dc = o
        return {
            "attn": z * 2 + lax.rem(c + dc, 2),
            "ffn": lax.rem(f + df, 4),
            "rep": lax.rem(r + dr, 4),
        }

    sib = {"attn": z * 2 + 1 - c}

    loads = []

    def load(src, dst):
        cp = pltpu.make_async_copy(src, dst, ld.at[len(loads)])
        cp.start()
        loads.append(cp)
        return cp

    sent = []
    groups = {}

    def remote(src, dst, send_sem, recv_sem, dev):
        return pltpu.make_async_remote_copy(
            src_ref=src, dst_ref=dst, send_sem=send_sem, recv_sem=recv_sem,
            device_id=dev, device_id_type=MESH,
        )

    def send(src, dst, dev, group=None, arrival=None):
        k = len(sent)
        if group is None:
            leave = ss.at[k]
        else:
            groups[group] = groups.get(group, 0) + 1
            leave = out_s.at[group]
        cp = remote(src, dst, leave, rs.at[k] if arrival is None else in_s.at[arrival], dev)
        cp.start()
        sent.append((group, cp))
        return cp

    def wait_in(blocks, arrival):
        remote(blocks, blocks, out_s.at[0], in_s.at[arrival], sib).wait_recv()

    l_q = load(q_h.at[0], qv)
    l_k = load(k_h.at[0], kv)
    l_v = load(v_h.at[0], vv)
    l_len = load(len_h, lenv)

    barrier = pltpu.get_barrier_semaphore()
    peers = [zdev(d) for d in (5, -5)] + [pdev(o) for o in PLANE]
    peers += [zdev(d) for d in (3, -3, 2, -2, 1, -1)]
    for dev in peers:
        pl.semaphore_signal(barrier, inc=1, device_id=dev, device_id_type=MESH)

    l_ids = load(ids_h, idsv)
    l_gw = load(gw_h, gwv)
    l_res = load(res_h.at[0], resv)
    l_gain = load(gain_h, gainv)
    half = pl.multiple_of(c * KH, KH)
    other = pl.multiple_of((1 - c) * KH, KH)
    l_wo = load(wo_h.at[:, pl.ds(half, KH)], wo.at[c, pl.ds(0, W)])
    l_wg = load(wg_h.at[c], wg.at[c, pl.ds(0, W)])
    l_wu = load(wu_h.at[c], wu.at[c, pl.ds(0, W)])
    l_wd = load(wd_h.at[c], wd.at[c, pl.ds(0, W)])

    l_q.wait()
    q32 = qv[...].astype(F32)
    for i in range(4):
        for h in range(16):
            qs[i * 16 + h : i * 16 + h + 1, :] = q32[i : i + 1, h * HD : (h + 1) * HD]
    l_k.wait()
    l_len.wait()
    l_v.wait()
    position = lax.broadcasted_iota(jnp.int32, (16, HD), 1)
    for i in range(4):
        s = mm(qs[i * 16 : (i + 1) * 16, :].astype(BF), kv[i], NT) * (HD**-0.5)
        s = jnp.where(position < lenv[0:1, i : i + 1], s, F32(-1e30))
        e = jnp.exp(s - jnp.max(s, axis=1, keepdims=True))
        p = (e / jnp.sum(e, axis=1, keepdims=True)).astype(BF)
        o = mm(p, vv[i])
        for h in range(16):
            hh, hg, j = h // 8, (h % 8) // 4, h % 4
            for k in range(2):
                row = hg * 8 + k * 4 + i
                att[hh, row : row + 1, j * HD : (j + 1) * HD] = o[h : h + 1, :]
    rowi = lax.broadcasted_iota(jnp.int32, (16, 1024), 0)
    mine = lax.rem(lax.div(rowi, 4), 2) == c
    xs[...] = jnp.where(mine, att[1 - c], 0.0).astype(BF)

    pl.semaphore_wait(barrier, len(peers))
    x_cp = send(xs, xr, sib)
    x_wo = send(wo_h.at[:, pl.ds(other, KH)], wo.at[c, pl.ds(0, W)], sib)
    x_wg = send(wg_h.at[1 - c], wg.at[c, pl.ds(0, W)], sib)
    x_wu = send(wu_h.at[1 - c], wu.at[c, pl.ds(0, W)], sib)
    x_wd = send(wd_h.at[1 - c], wd.at[c, pl.ds(0, W)], sib)

    def gather_z(buf, group):
        got = {}

        def pass_on(o):
            block = buf.at[zidx(-o)]
            for to in RELAY[abs(o)]:
                if o == 0:
                    got[to] = send(block, block, zdev(to), group)
                    got[-to] = send(block, block, zdev(-to), group)
                elif to < 8:
                    sgn = 1 if o > 0 else -1
                    arrival = 2 * group + (sgn * to in LAST)
                    send(block, block, zdev(sgn * to - o), group, arrival)

        pass_on(0)
        yield
        for sgn in (1, -1):
            got[sgn].wait_recv()
            pass_on(sgn)
        yield
        got[5].wait_recv()
        got[-5].wait_recv()
        far = buf.at[zidx(-5 * sg)]
        send(far, far, zdev(3 * sg), group, 2 * group + 1)
        pass_on(5)
        pass_on(-5)
        yield
        wait_in(buf.at[pl.ds(0, len(MIDDLE) - 2)], 2 * group)
        yield
        wait_in(buf.at[pl.ds(0, len(LAST))], 2 * group + 1)

    x_cp.wait_recv()
    ag1[z] = jnp.where(mine, att[c], 0.0).astype(BF) + xr[...]
    heads = gather_z(ag1, 0)
    next(heads)

    for buf in (wo, wg, wu, wd):
        buf[:, W:WP, :] = jnp.zeros((2, WP - W, buf.shape[2]), BF)
    l_res.wait()
    l_gain.wait()
    l_ids.wait()
    l_gw.wait()
    pad32[...] = jnp.zeros((ROWS, WP), F32)
    pad32[:, 0:W] = resv[...].astype(F32)
    pad1[...] = jnp.zeros((1, WP), F32)
    pad1[:, 0:W] = gainv[...]
    spot = lax.broadcasted_iota(jnp.int32, (128, ROWS), 0)
    hits = jnp.zeros((128, ROWS), F32)
    share = jnp.zeros((128, ROWS), F32)
    for k in range(3):
        same = idsv[k] == lax.div(spot, SLOT)
        hits = hits + jnp.where(same, 1.0, 0.0)
        share = share + jnp.where(same, gwv[k], 0.0)
    earlier = lax.broadcasted_iota(jnp.int32, (ROWS, ROWS), 0) < lax.broadcasted_iota(
        jnp.int32, (ROWS, ROWS), 1
    )
    before = mm(hits.astype(BF), jnp.where(earlier, 1.0, 0.0).astype(BF))
    placed = before == lax.rem(spot, SLOT).astype(F32)
    pick = jnp.where(placed, hits, 0.0).astype(BF)
    share = jnp.where(placed, share, 0.0)
    eye = lax.broadcasted_iota(jnp.int32, (ROWS, ROWS), 0) == lax.broadcasted_iota(
        jnp.int32, (ROWS, ROWS), 1
    )
    eye = jnp.where(eye, 1.0, 0.0).astype(BF)
    share_hi = share.astype(BF)
    share_lo = (share - share_hi.astype(F32)).astype(BF)
    share_hi = jnp.concatenate([mm(eye, share_hi, NT).astype(BF)] * 4, axis=1)
    share_lo = jnp.concatenate([mm(eye, share_lo, NT).astype(BF)] * 4, axis=1)


    for _ in heads:
        pass
    l_wo.wait()
    x_wo.wait_recv()

    rows = ag1[...].reshape(CHIPS * 16, 1024)
    for s in range(2):
        p0 = mm(rows, wo[s, :, 0:1024], NT).reshape(CHIPS, 16, WP)
        p1 = mm(rows, wo[s, :, 1024:2048], NT).reshape(CHIPS, 16, WP)
        u = p0[:, 0:8] + p1[:, 8:16]
        us[s] = u.reshape(4, ROWS, WP).astype(BF)
    for df, dc in XCORE:
        q = lax.rem(f + df, 4)
        s = lax.rem(c + dc, 2)
        send(us.at[s, q], rb.at[f * 2 + c], pdev((df, 0, dc)), 3, 6)
    rb[f * 2 + c] = us[c, f]
    hidden = pad32[...]
    wait_in(rb.at[pl.ds(0, 7)], 6)
    for k in range(8):
        hidden = hidden + rb[k].astype(F32)
    hid = hidden.astype(BF).astype(F32)
    squares = jnp.sum(hid * hid, axis=1, keepdims=True)
    sq_hi = squares.astype(BF).astype(F32)
    lane2 = lax.broadcasted_iota(jnp.int32, (ROWS, WP), 1)
    normed = jnp.where(
        lane2 == W, sq_hi, jnp.where(lane2 == W + 1, squares - sq_hi, hid * pad1[...])
    ).astype(BF)
    tok[...] = mm(pick, normed).astype(BF).reshape(8, SLOT, WP)

    for o in PLANE:
        e = lax.rem(f + o[0], 4) * 2 + lax.rem(c + o[2], 2)
        send(tok.at[e], xb.at[c * 16 + r * 4 + f], pdev(o), 4, 7)
    xb[c * 16 + r * 4 + f] = tok[f * 2 + c]
    l_wg.wait()
    x_wg.wait_recv()
    l_wu.wait()
    x_wu.wait_recv()
    wait_in(xb.at[pl.ds(0, 31)], 7)
    x0 = xb[0:16].reshape(256, WP)
    x1 = xb[16:32].reshape(256, WP)
    ones = lax.broadcasted_iota(jnp.int32, (16, WP), 1)
    ones = jnp.where((ones == W) | (ones == W + 1), 1.0, 0.0).astype(BF)
    sq = (mm(ones, x0, NT) + mm(ones, x1, NT))[0:1, :]
    sq_hi = sq.astype(BF).astype(F32)
    sq_lo = sq - sq_hi
    def project(w, lo, hi):
        out = mm(x0, w[0, :, lo:hi]) + mm(x1, w[1, :, lo:hi])
        return out.reshape(CHIPS, SLOT, hi - lo)

    tail = project(wu, TAIL, EFF)
    slot = lax.broadcasted_iota(jnp.int32, (CHIPS, SLOT, 128), 1)

    def put(buf, column, base, first_tile):
        for j in range(base.shape[2] // 128):
            t = first_tile + j
            if t in (2, 3):
                low = sq_hi[:, (t - 2) * 128 : (t - 1) * 128].reshape(1, 1, 128)
            elif t in (4, 5):
                low = sq_lo[:, (t - 4) * 128 : (t - 3) * 128].reshape(1, 1, 128)
            else:
                k = 9 + t if t < 2 else 5 + t
                low = tail[:, k : k + 1, :]
            piece = jnp.where(slot == CAP + 1, low, base[:, :, j * 128 : (j + 1) * 128])
            piece = jnp.where(slot == CAP, tail[:, t : t + 1, :], piece)
            buf[:, :, column + j * 128 : column + (j + 1) * 128] = piece.astype(BF)

    sides = ((0, 1), (1, -1))

    class Sum:
        def __init__(self, pb, r1, s2, r2, group):
            self.pb, self.r1, self.s2, self.r2 = pb, r1, s2, r2
            self.group, self.arrival = group, 8 + 3 * (group - 5)

        def leaves(self):
            slots = ((7, -1, 0), (5, 1, 2), (8, 0, 4), (4, -2, 5), (3, -1, 7), (1, 1, 9))
            for o, d, k in slots:
                arrival = self.arrival + (k > 4)
                if o == 8:
                    send(self.pb.at[zidx(8)], self.r1.at[k], zdev(-2 * sg), self.group, arrival)
                    continue
                for side, sgn in sides:
                    src = self.pb.at[zidx(-sgn * o)]
                    send(src, self.r1.at[k + side], zdev(sgn * d), self.group, arrival)

        def relay(self, slot, o, first, last):
            wait_in(self.r1.at[pl.ds(first, last - first)], self.arrival + slot)
            for side, sgn in sides:
                acc = self.pb[zidx(-sgn * o)].astype(F32)
                for k in range(first + side, min(last, first + 4) if o == 6 else last, 2):
                    acc = acc + self.r1[k].astype(F32)
                if o == 6:
                    acc = acc + jnp.where(c == side, self.r1[4].astype(F32), 0.0)
                k = 2 * slot + side
                self.s2[k] = acc.astype(BF)
                send(self.s2.at[k], self.r2.at[k], zdev(-sgn * o), self.group, self.arrival + 2)

        def total(self):
            wait_in(self.r2, self.arrival + 2)
            out = self.pb[z].astype(F32)
            for k in range(4):
                out = out + self.r2[k].astype(F32)
            return out

    sum_a, sum_b = Sum(pb_a, r1_a, s2_a, r2_a, 5), Sum(pb_b, r1_b, s2_b, r2_b, 6)
    put(pb_a, 0, project(wg, 0, EA), 0)
    put(pb_a, EA, project(wu, 0, EA), 3)
    sum_a.leaves()
    put(pb_b, 0, project(wg, EA, EFF), 6)
    put(pb_b, EB, project(wu, EA, TAIL), 8)
    sum_b.leaves()
    sum_a.relay(0, 6, 0, 5)
    sum_b.relay(0, 6, 0, 5)
    sum_a.relay(1, 2, 5, 11)
    sum_b.relay(1, 2, 5, 11)

    def activate(gate, up):
        gate, up = gate * rinv, up * rinv
        act = gate / (1.0 + jnp.exp(-gate)) * up
        live = lax.broadcasted_iota(jnp.int32, act.shape, 0) < CAP
        return jnp.where(live, act, 0.0).astype(BF)

    total = sum_a.total()
    for t in range(6):
        last_up[t : t + 1, :] = total[CAP : CAP + 1, t * 128 : (t + 1) * 128]
    for t in range(2):
        last_up[9 + t : 10 + t, :] = total[CAP + 1 : CAP + 2, t * 128 : (t + 1) * 128]
    sq = total[CAP + 1 : CAP + 2, 256:512] + total[CAP + 1 : CAP + 2, 512:768]
    row = lax.broadcasted_iota(jnp.int32, (SLOT, 256), 0)
    lane3 = lax.broadcasted_iota(jnp.int32, (SLOT, 256), 1)
    sq = jnp.sum(jnp.where(lane3 == z * SLOT + row, sq, 0.0), axis=1, keepdims=True)
    rinv = lax.rsqrt(sq / D + 1e-6)
    ag2_a[z] = activate(total[:, 0:EA], total[:, EA : 2 * EA])
    rows_a = gather_z(ag2_a, 1)
    next(rows_a)
    total = sum_b.total()
    for t in range(3):
        last_up[6 + t : 7 + t, :] = total[CAP : CAP + 1, t * 128 : (t + 1) * 128]
        last_up[11 + t : 12 + t, :] = total[CAP + 1 : CAP + 2, t * 128 : (t + 1) * 128]
    last_up[CAP:SLOT, :] = jnp.zeros((SLOT - CAP, 128), F32)
    up = jnp.concatenate([total[:, EB : EB + 128], last_up[...]], axis=1)
    ag2_b[z] = activate(total[:, 0:EB], up)
    rows_b = gather_z(ag2_b, 2)
    next(rows_b)

    l_wd.wait()
    x_wd.wait_recv()
    me = r * 8 + f * 2 + c
    stay = []

    def give_back(offsets):
        first = len(stay)
        act_a = jnp.concatenate([ag2_a[zidx(-o)] for o in offsets], axis=0)
        act_b = jnp.concatenate([ag2_b[zidx(-o)] for o in offsets], axis=0)
        for s in range(2):
            out = mm(act_a, wd[s, :, 0:EA], NT) + mm(act_b, wd[s, :, EA:EFF], NT)
            eb[s, first : first + len(offsets)] = out.astype(BF).reshape(len(offsets), SLOT, WP)
        for k, o in enumerate(offsets):
            b = zidx(-o)
            fo, ro = lax.rem(b, 4), lax.div(b, 4)
            i = first + k
            stay.append(i)
            dev = {"attn": z * 2 + 1 - c, "ffn": fo, "rep": ro}
            send(eb.at[1 - c, i], rr.at[me], dev, 7, 14)
            away = b != r * 4 + f

            @pl.when(away)
            def _():
                dev = {"attn": z * 2 + c, "ffn": fo, "rep": ro}
                remote(eb.at[c, i], rr.at[me], out_s.at[7], in_s.at[14], dev).start()

            @pl.when(jnp.logical_not(away))
            def _():
                rr[me] = eb[c, i]

    next(rows_a)
    next(rows_b)
    next(rows_a)
    give_back(FIRST)
    next(rows_b)
    next(rows_a)
    next(rows_b)
    give_back(MIDDLE)
    for rows in (rows_a, rows_b):
        for _ in rows:
            pass
    give_back(LAST)
    wait_in(rr.at[pl.ds(0, 31)], 14)
    back = rr[...].reshape(512, WP)
    mixed = hidden + mm(share_hi, back) + mm(share_lo, back)
    out_ref[0] = mixed[:, 0:W]
    for group, cp in sent:
        if group is None:
            cp.wait_send()
    groups[7] = 31
    whole = {0: ag1, 1: ag2_a, 2: ag2_b, 3: rb, 4: xb, 5: pb_a, 6: pb_b, 7: rr}
    for group, n in groups.items():
        blocks = whole[group].at[pl.ds(0, n)]
        remote(blocks, blocks, out_s.at[group], in_s.at[0], sib).wait_send()


N_SENT = 5 + 15 + 7 + 31 + 30 + 30 + 16


def per_device(q, k, v, lens, wo, res, gain, ids, gw, wg, wu, wd):
    ids = jnp.transpose(ids, (2, 0, 1))
    gw = jnp.transpose(gw, (2, 0, 1))
    any_spec = pl.BlockSpec(memory_space=pl.ANY)
    vm = pltpu.VMEM
    dma = pltpu.SemaphoreType.DMA
    return pl.pallas_call(
        kernel,
        name="layer",
        out_shape=pltpu.VMEM((1, ROWS, W), F32),
        in_specs=[any_spec] * 12,
        out_specs=pl.BlockSpec(memory_space=pltpu.VMEM),
        scratch_shapes=[
            vm((4, 4096), BF),
            vm((4, 256, HD), BF),
            vm((4, 256, HD), BF),
            vm((1, 4), jnp.int32),
            vm((ROWS, W), BF),
            vm((1, W), F32),
            vm((3, 1, ROWS), jnp.int32),
            vm((3, 1, ROWS), F32),
            vm((2, WP, KH), BF),
            vm((2, WP, EFF), BF),
            vm((2, WP, EFF), BF),
            vm((2, WP, EFF), BF),
            vm((64, HD), F32),
            vm((2, 16, 1024), F32),
            vm((16, 1024), BF),
            vm((16, 1024), BF),
            vm((CHIPS, 16, 1024), BF),
            vm((2, 4, ROWS, WP), BF),
            vm((8, ROWS, WP), BF),
            vm((ROWS, WP), F32),
            vm((1, WP), F32),
            vm((8, SLOT, WP), BF),
            vm((32, SLOT, WP), BF),
            vm((CHIPS, SLOT, 2 * EA), BF),
            vm((11, SLOT, 2 * EA), BF),
            vm((4, SLOT, 2 * EA), BF),
            vm((4, SLOT, 2 * EA), BF),
            vm((CHIPS, SLOT, EB + 128), BF),
            vm((11, SLOT, EB + 128), BF),
            vm((4, SLOT, EB + 128), BF),
            vm((4, SLOT, EB + 128), BF),
            vm((SLOT, 128), F32),
            vm((CHIPS, SLOT, EA), BF),
            vm((CHIPS, SLOT, EB), BF),
            vm((2, 16, SLOT, WP), BF),
            vm((32, SLOT, WP), BF),
            dma((12,)),
            dma((N_SENT,)),
            dma((N_SENT,)),
            dma((8,)),
            dma((15,)),
        ],
        compiler_params=pltpu.CompilerParams(
            collective_id=0, has_side_effects=True, vmem_limit_bytes=56 * 1024 * 1024
        ),
    )(q, k, v, lens, wo, res, gain.reshape(1, W), ids, gw, wg, wu, wd)


def solution(mesh):
    in_specs = (
        P("rep", "attn", "ffn"),
        P("rep", "attn", None, None),
        P("rep", "attn", None, None),
        P("rep", "attn"),
        P("attn", "ffn"),
        P("rep", "ffn", "attn"),
        P("attn"),
        P("rep", "ffn", None),
        P("rep", "ffn", None),
        P("ffn", "attn", "rep"),
        P("ffn", "attn", "rep"),
        P("ffn", "attn", "rep"),
    )
    out_specs = P("rep", "ffn", "attn")
    return jax.shard_map(
        per_device, mesh=mesh, in_specs=in_specs, out_specs=out_specs, check_vma=False
    )
```

```python
import functools

import jax
import jax.numpy as jnp
from jax import lax
from jax.experimental import pallas as pl
from jax.experimental.pallas import tpu as pltpu
from jax.sharding import PartitionSpec as P

MESH = pl.DeviceIdType.MESH
BF = jnp.bfloat16
F32 = jnp.float32
NT = (((1,), (1,)), ((), ()))
NN = (((1,), (0,)), ((), ()))

CHIPS = 16
SIDE = 4
W = 224
WP = 256
CAP = 14
SLOT = 16
ROWS = 32
EFF = 640
EA, EB = 384, 256
TAIL = 512
HD = 256
KH = 2048
D = 7168

PLANE = sorted(
    ((df, dr, dc) for df in range(4) for dr in range(4) for dc in range(2) if df or dr or dc),
    key=lambda o: (-(min(o[0], 4 - o[0]) + min(o[1], 4 - o[1])), o),
)
XCORE = sorted(
    ((df, dc) for df in range(4) for dc in range(2) if df or dc),
    key=lambda o: (-min(o[0], 4 - o[0]), o),
)

FIRST = (0, 1, -1)
MIDDLE = (5, -5, 2, -2, 3, -3, 4, -4)
LAST = (6, -6, 7, -7, 8)
RELAY = {0: (5, 1), 1: (4, 3, 2), 5: (8, 7, 6)}


def mm(a, b, dims=NN):
    return lax.dot_general(a, b, dims, preferred_element_type=F32)


def kernel(
    q_h, k_h, v_h, len_h, wo_h, res_h, gain_h, ids_h, gw_h, wg_h, wu_h, wd_h,
    out_ref,
    qv, kv, vv, lenv, resv, gainv, idsv, gwv, wo, wg, wu, wd,
    qs, att, xs, xr, ag1, ag1b, us, rb, pad32, pad1, tok, xb, pb_a, r1_a, s2_a, r2_a, pb_b, r1_b, s2_b, r2_b, last_up, ag2_a, ag2_b, eb, rr,
    ld, ss, rs, out_s, in_s,
):
    a = lax.axis_index("attn")
    f = lax.axis_index("ffn")
    r = lax.axis_index("rep")
    c = lax.rem(a, 2)
    z = lax.div(a, 2)
    sg = 1 - 2 * c

    def zdev(d):
        return {"attn": lax.rem(z + d + CHIPS, CHIPS) * 2 + c}

    def zidx(d):
        return lax.rem(z + d + 2 * CHIPS, CHIPS)

    def pdev(o):
        df, dr, dc = o
        return {
            "attn": z * 2 + lax.rem(c + dc, 2),
            "ffn": lax.rem(f + df, 4),
            "rep": lax.rem(r + dr, 4),
        }

    sib = {"attn": z * 2 + 1 - c}

    loads = []

    def load(src, dst):
        cp = pltpu.make_async_copy(src, dst, ld.at[len(loads)])
        cp.start()
        loads.append(cp)
        return cp

    sent = []
    groups = {}

    def remote(src, dst, send_sem, recv_sem, dev):
        return pltpu.make_async_remote_copy(
            src_ref=src, dst_ref=dst, send_sem=send_sem, recv_sem=recv_sem,
            device_id=dev, device_id_type=MESH,
        )

    def send(src, dst, dev, group=None, arrival=None):
        k = len(sent)
        if group is None:
            leave = ss.at[k]
        else:
            groups[group] = groups.get(group, 0) + 1
            leave = out_s.at[group]
        cp = remote(src, dst, leave, rs.at[k] if arrival is None else in_s.at[arrival], dev)
        cp.start()
        sent.append((group, cp))
        return cp

    def wait_in(blocks, arrival):
        remote(blocks, blocks, out_s.at[0], in_s.at[arrival], sib).wait_recv()

    l_q = load(q_h.at[0], qv)
    l_k = load(k_h.at[0], kv)
    l_v = load(v_h.at[0], vv)
    l_len = load(len_h, lenv)

    barrier = pltpu.get_barrier_semaphore()
    peers = [zdev(d) for d in (5, -5)] + [pdev(o) for o in PLANE]
    peers += [zdev(d) for d in (3, -3, 2, -2, 1, -1)]
    for dev in peers:
        pl.semaphore_signal(barrier, inc=1, device_id=dev, device_id_type=MESH)

    l_ids = load(ids_h, idsv)
    l_gw = load(gw_h, gwv)
    l_res = load(res_h.at[0], resv)
    l_gain = load(gain_h, gainv)
    half = pl.multiple_of(c * KH, KH)
    other = pl.multiple_of((1 - c) * KH, KH)
    l_wo = load(wo_h.at[:, pl.ds(half, KH)], wo.at[c, pl.ds(0, W)])
    l_wg = load(wg_h.at[c], wg.at[c, pl.ds(0, W)])
    l_wu = load(wu_h.at[c], wu.at[c, pl.ds(0, W)])
    l_wd = load(wd_h.at[c], wd.at[c, pl.ds(0, W)])

    l_q.wait()
    q32 = qv[...].astype(F32)
    for i in range(4):
        for h in range(16):
            qs[i * 16 + h : i * 16 + h + 1, :] = q32[i : i + 1, h * HD : (h + 1) * HD]
    l_k.wait()
    l_len.wait()
    l_v.wait()
    position = lax.broadcasted_iota(jnp.int32, (16, HD), 1)
    for i in range(4):
        s = mm(qs[i * 16 : (i + 1) * 16, :].astype(BF), kv[i], NT) * (HD**-0.5)
        s = jnp.where(position < lenv[0:1, i : i + 1], s, F32(-1e30))
        e = jnp.exp(s - jnp.max(s, axis=1, keepdims=True))
        p = (e / jnp.sum(e, axis=1, keepdims=True)).astype(BF)
        o = mm(p, vv[i])
        for h in range(16):
            hh, hg, j = h // 8, (h % 8) // 4, h % 4
            for k in range(2):
                row = hg * 8 + k * 4 + i
                att[hh, row : row + 1, j * HD : (j + 1) * HD] = o[h : h + 1, :]
    rowi = lax.broadcasted_iota(jnp.int32, (16, 1024), 0)
    mine = lax.rem(lax.div(rowi, 4), 2) == c
    xs[...] = jnp.where(mine, att[1 - c], 0.0).astype(BF)

    pl.semaphore_wait(barrier, len(peers))
    x_cp = send(xs, xr, sib)
    x_wo = send(wo_h.at[:, pl.ds(other, KH)], wo.at[c, pl.ds(0, W)], sib)
    x_wg = send(wg_h.at[1 - c], wg.at[c, pl.ds(0, W)], sib)
    x_wu = send(wu_h.at[1 - c], wu.at[c, pl.ds(0, W)], sib)
    x_wd = send(wd_h.at[1 - c], wd.at[c, pl.ds(0, W)], sib)

    def gather_z(buf, group):
        got = {}

        def pass_on(o):
            block = buf.at[zidx(-o)]
            for to in RELAY[abs(o)]:
                if o == 0:
                    got[to] = send(block, block, zdev(to), group)
                    got[-to] = send(block, block, zdev(-to), group)
                elif to < 8:
                    sgn = 1 if o > 0 else -1
                    arrival = 2 * group + (sgn * to in LAST)
                    send(block, block, zdev(sgn * to - o), group, arrival)

        pass_on(0)
        yield
        for sgn in (1, -1):
            got[sgn].wait_recv()
            pass_on(sgn)
        yield
        got[5].wait_recv()
        got[-5].wait_recv()
        far = buf.at[zidx(-5 * sg)]
        send(far, far, zdev(3 * sg), group, 2 * group + 1)
        pass_on(5)
        pass_on(-5)
        yield
        wait_in(buf.at[pl.ds(0, len(MIDDLE) - 2)], 2 * group)
        yield
        wait_in(buf.at[pl.ds(0, len(LAST))], 2 * group + 1)

    x_cp.wait_recv()
    whole_block = jnp.where(mine, att[c], 0.0).astype(BF) + xr[...]
    ag1[z] = whole_block[:, 0:512]
    ag1b[z] = whole_block[:, 512:1024]
    heads = gather_z(ag1, 0)
    heads_b = gather_z(ag1b, 8)
    next(heads)
    next(heads_b)

    for buf in (wo, wg, wu, wd):
        buf[:, W:WP, :] = jnp.zeros((2, WP - W, buf.shape[2]), BF)
    l_res.wait()
    l_gain.wait()
    l_ids.wait()
    l_gw.wait()
    pad32[...] = jnp.zeros((ROWS, WP), F32)
    pad32[:, 0:W] = resv[...].astype(F32)
    pad1[...] = jnp.zeros((1, WP), F32)
    pad1[:, 0:W] = gainv[...]
    spot = lax.broadcasted_iota(jnp.int32, (128, ROWS), 0)
    hits = jnp.zeros((128, ROWS), F32)
    share = jnp.zeros((128, ROWS), F32)
    for k in range(3):
        same = idsv[k] == lax.div(spot, SLOT)
        hits = hits + jnp.where(same, 1.0, 0.0)
        share = share + jnp.where(same, gwv[k], 0.0)
    earlier = lax.broadcasted_iota(jnp.int32, (ROWS, ROWS), 0) < lax.broadcasted_iota(
        jnp.int32, (ROWS, ROWS), 1
    )
    before = mm(hits.astype(BF), jnp.where(earlier, 1.0, 0.0).astype(BF))
    placed = before == lax.rem(spot, SLOT).astype(F32)
    pick = jnp.where(placed, hits, 0.0).astype(BF)
    share = jnp.where(placed, share, 0.0)
    eye = lax.broadcasted_iota(jnp.int32, (ROWS, ROWS), 0) == lax.broadcasted_iota(
        jnp.int32, (ROWS, ROWS), 1
    )
    eye = jnp.where(eye, 1.0, 0.0).astype(BF)
    share_hi = share.astype(BF)
    share_lo = (share - share_hi.astype(F32)).astype(BF)
    share_hi = jnp.concatenate([mm(eye, share_hi, NT).astype(BF)] * 4, axis=1)
    share_lo = jnp.concatenate([mm(eye, share_lo, NT).astype(BF)] * 4, axis=1)


    for _ in range(2):
        next(heads)
        next(heads_b)
    for it in (heads, heads_b):
        for _ in it:
            pass
    l_wo.wait()
    x_wo.wait_recv()

    rows = ag1[...].reshape(CHIPS * 16, 512)
    rows_b = ag1b[...].reshape(CHIPS * 16, 512)
    for s in range(2):
        p0 = mm(rows, wo[s, :, 0:512], NT) + mm(rows_b, wo[s, :, 512:1024], NT)
        p1 = mm(rows, wo[s, :, 1024:1536], NT) + mm(rows_b, wo[s, :, 1536:2048], NT)
        p0, p1 = p0.reshape(CHIPS, 16, WP), p1.reshape(CHIPS, 16, WP)
        u = p0[:, 0:8] + p1[:, 8:16]
        us[s] = u.reshape(4, ROWS, WP).astype(BF)
    for df, dc in XCORE:
        q = lax.rem(f + df, 4)
        s = lax.rem(c + dc, 2)
        send(us.at[s, q], rb.at[f * 2 + c], pdev((df, 0, dc)), 3, 6)
    rb[f * 2 + c] = us[c, f]
    hidden = pad32[...]
    wait_in(rb.at[pl.ds(0, 7)], 6)
    for k in range(8):
        hidden = hidden + rb[k].astype(F32)
    hid = hidden.astype(BF).astype(F32)
    squares = jnp.sum(hid * hid, axis=1, keepdims=True)
    sq_hi = squares.astype(BF).astype(F32)
    lane2 = lax.broadcasted_iota(jnp.int32, (ROWS, WP), 1)
    normed = jnp.where(
        lane2 == W, sq_hi, jnp.where(lane2 == W + 1, squares - sq_hi, hid * pad1[...])
    ).astype(BF)
    tok[...] = mm(pick, normed).astype(BF).reshape(8, SLOT, WP)

    for o in PLANE:
        e = lax.rem(f + o[0], 4) * 2 + lax.rem(c + o[2], 2)
        send(tok.at[e], xb.at[c * 16 + r * 4 + f], pdev(o), 4, 7)
    xb[c * 16 + r * 4 + f] = tok[f * 2 + c]
    l_wg.wait()
    x_wg.wait_recv()
    l_wu.wait()
    x_wu.wait_recv()
    wait_in(xb.at[pl.ds(0, 31)], 7)
    x0 = xb[0:16].reshape(256, WP)
    x1 = xb[16:32].reshape(256, WP)
    ones = lax.broadcasted_iota(jnp.int32, (16, WP), 1)
    ones = jnp.where((ones == W) | (ones == W + 1), 1.0, 0.0).astype(BF)
    sq = (mm(ones, x0, NT) + mm(ones, x1, NT))[0:1, :]
    sq_hi = sq.astype(BF).astype(F32)
    sq_lo = sq - sq_hi
    def project(w, lo, hi):
        out = mm(x0, w[0, :, lo:hi]) + mm(x1, w[1, :, lo:hi])
        return out.reshape(CHIPS, SLOT, hi - lo)

    tail = project(wu, TAIL, EFF)
    slot = lax.broadcasted_iota(jnp.int32, (CHIPS, SLOT, 128), 1)

    def put(buf, column, base, first_tile):
        for j in range(base.shape[2] // 128):
            t = first_tile + j
            if t in (2, 3):
                low = sq_hi[:, (t - 2) * 128 : (t - 1) * 128].reshape(1, 1, 128)
            elif t in (4, 5):
                low = sq_lo[:, (t - 4) * 128 : (t - 3) * 128].reshape(1, 1, 128)
            else:
                k = 9 + t if t < 2 else 5 + t
                low = tail[:, k : k + 1, :]
            piece = jnp.where(slot == CAP + 1, low, base[:, :, j * 128 : (j + 1) * 128])
            piece = jnp.where(slot == CAP, tail[:, t : t + 1, :], piece)
            buf[:, :, column + j * 128 : column + (j + 1) * 128] = piece.astype(BF)

    sides = ((0, 1), (1, -1))

    class Sum:
        def __init__(self, pb, r1, s2, r2, group):
            self.pb, self.r1, self.s2, self.r2 = pb, r1, s2, r2
            self.group, self.arrival = group, 8 + 3 * (group - 5)

        def leaves(self):
            slots = ((7, -1, 0), (5, 1, 2), (8, 0, 4), (4, -2, 5), (3, -1, 7), (1, 1, 9))
            for o, d, k in slots:
                arrival = self.arrival + (k > 4)
                if o == 8:
                    send(self.pb.at[zidx(8)], self.r1.at[k], zdev(-2 * sg), self.group, arrival)
                    continue
                for side, sgn in sides:
                    src = self.pb.at[zidx(-sgn * o)]
                    send(src, self.r1.at[k + side], zdev(sgn * d), self.group, arrival)

        def relay(self, slot, o, first, last):
            wait_in(self.r1.at[pl.ds(first, last - first)], self.arrival + slot)
            for side, sgn in sides:
                acc = self.pb[zidx(-sgn * o)].astype(F32)
                for k in range(first + side, min(last, first + 4) if o == 6 else last, 2):
                    acc = acc + self.r1[k].astype(F32)
                if o == 6:
                    acc = acc + jnp.where(c == side, self.r1[4].astype(F32), 0.0)
                k = 2 * slot + side
                self.s2[k] = acc.astype(BF)
                send(self.s2.at[k], self.r2.at[k], zdev(-sgn * o), self.group, self.arrival + 2)

        def total(self):
            wait_in(self.r2, self.arrival + 2)
            out = self.pb[z].astype(F32)
            for k in range(4):
                out = out + self.r2[k].astype(F32)
            return out

    sum_a, sum_b = Sum(pb_a, r1_a, s2_a, r2_a, 5), Sum(pb_b, r1_b, s2_b, r2_b, 6)
    put(pb_a, 0, project(wg, 0, EA), 0)
    put(pb_a, EA, project(wu, 0, EA), 3)
    sum_a.leaves()
    put(pb_b, 0, project(wg, EA, EFF), 6)
    put(pb_b, EB, project(wu, EA, TAIL), 8)
    sum_b.leaves()
    sum_a.relay(0, 6, 0, 5)
    sum_b.relay(0, 6, 0, 5)
    sum_a.relay(1, 2, 5, 11)
    sum_b.relay(1, 2, 5, 11)

    def activate(gate, up):
        gate, up = gate * rinv, up * rinv
        act = gate / (1.0 + jnp.exp(-gate)) * up
        live = lax.broadcasted_iota(jnp.int32, act.shape, 0) < CAP
        return jnp.where(live, act, 0.0).astype(BF)

    total = sum_a.total()
    for t in range(6):
        last_up[t : t + 1, :] = total[CAP : CAP + 1, t * 128 : (t + 1) * 128]
    for t in range(2):
        last_up[9 + t : 10 + t, :] = total[CAP + 1 : CAP + 2, t * 128 : (t + 1) * 128]
    sq = total[CAP + 1 : CAP + 2, 256:512] + total[CAP + 1 : CAP + 2, 512:768]
    row = lax.broadcasted_iota(jnp.int32, (SLOT, 256), 0)
    lane3 = lax.broadcasted_iota(jnp.int32, (SLOT, 256), 1)
    sq = jnp.sum(jnp.where(lane3 == z * SLOT + row, sq, 0.0), axis=1, keepdims=True)
    rinv = lax.rsqrt(sq / D + 1e-6)
    ag2_a[z] = activate(total[:, 0:EA], total[:, EA : 2 * EA])
    rows_a = gather_z(ag2_a, 1)
    next(rows_a)
    total = sum_b.total()
    for t in range(3):
        last_up[6 + t : 7 + t, :] = total[CAP : CAP + 1, t * 128 : (t + 1) * 128]
        last_up[11 + t : 12 + t, :] = total[CAP + 1 : CAP + 2, t * 128 : (t + 1) * 128]
    last_up[CAP:SLOT, :] = jnp.zeros((SLOT - CAP, 128), F32)
    up = jnp.concatenate([total[:, EB : EB + 128], last_up[...]], axis=1)
    ag2_b[z] = activate(total[:, 0:EB], up)
    rows_b = gather_z(ag2_b, 2)
    next(rows_b)

    l_wd.wait()
    x_wd.wait_recv()
    me = r * 8 + f * 2 + c
    stay = []

    def give_back(offsets):
        first = len(stay)
        act_a = jnp.concatenate([ag2_a[zidx(-o)] for o in offsets], axis=0)
        act_b = jnp.concatenate([ag2_b[zidx(-o)] for o in offsets], axis=0)
        for s in range(2):
            out = mm(act_a, wd[s, :, 0:EA], NT) + mm(act_b, wd[s, :, EA:EFF], NT)
            eb[s, first : first + len(offsets)] = out.astype(BF).reshape(len(offsets), SLOT, WP)
        for k, o in enumerate(offsets):
            b = zidx(-o)
            fo, ro = lax.rem(b, 4), lax.div(b, 4)
            i = first + k
            stay.append(i)
            dev = {"attn": z * 2 + 1 - c, "ffn": fo, "rep": ro}
            send(eb.at[1 - c, i], rr.at[me], dev, 7, 14)
            away = b != r * 4 + f

            @pl.when(away)
            def _():
                dev = {"attn": z * 2 + c, "ffn": fo, "rep": ro}
                remote(eb.at[c, i], rr.at[me], out_s.at[7], in_s.at[14], dev).start()

            @pl.when(jnp.logical_not(away))
            def _():
                rr[me] = eb[c, i]

    next(rows_a)
    next(rows_b)
    next(rows_a)
    give_back(FIRST)
    next(rows_b)
    next(rows_a)
    next(rows_b)
    give_back(MIDDLE)
    for rows in (rows_a, rows_b):
        for _ in rows:
            pass
    give_back(LAST)
    wait_in(rr.at[pl.ds(0, 31)], 14)
    back = rr[...].reshape(512, WP)
    mixed = hidden + mm(share_hi, back) + mm(share_lo, back)
    out_ref[0] = mixed[:, 0:W]
    for group, cp in sent:
        if group is None:
            cp.wait_send()
    groups[7] = 31
    whole = {8: ag1b, 0: ag1, 1: ag2_a, 2: ag2_b, 3: rb, 4: xb, 5: pb_a, 6: pb_b, 7: rr}
    for group, n in groups.items():
        blocks = whole[group].at[pl.ds(0, n)]
        remote(blocks, blocks, out_s.at[group], in_s.at[0], sib).wait_send()


N_SENT = 5 + 30 + 7 + 31 + 30 + 30 + 16


def per_device(q, k, v, lens, wo, res, gain, ids, gw, wg, wu, wd):
    ids = jnp.transpose(ids, (2, 0, 1))
    gw = jnp.transpose(gw, (2, 0, 1))
    any_spec = pl.BlockSpec(memory_space=pl.ANY)
    vm = pltpu.VMEM
    dma = pltpu.SemaphoreType.DMA
    return pl.pallas_call(
        kernel,
        name="layer",
        out_shape=pltpu.VMEM((1, ROWS, W), F32),
        in_specs=[any_spec] * 12,
        out_specs=pl.BlockSpec(memory_space=pltpu.VMEM),
        scratch_shapes=[
            vm((4, 4096), BF),
            vm((4, 256, HD), BF),
            vm((4, 256, HD), BF),
            vm((1, 4), jnp.int32),
            vm((ROWS, W), BF),
            vm((1, W), F32),
            vm((3, 1, ROWS), jnp.int32),
            vm((3, 1, ROWS), F32),
            vm((2, WP, KH), BF),
            vm((2, WP, EFF), BF),
            vm((2, WP, EFF), BF),
            vm((2, WP, EFF), BF),
            vm((64, HD), F32),
            vm((2, 16, 1024), F32),
            vm((16, 1024), BF),
            vm((16, 1024), BF),
            vm((CHIPS, 16, 512), BF),
            vm((CHIPS, 16, 512), BF),
            vm((2, 4, ROWS, WP), BF),
            vm((8, ROWS, WP), BF),
            vm((ROWS, WP), F32),
            vm((1, WP), F32),
            vm((8, SLOT, WP), BF),
            vm((32, SLOT, WP), BF),
            vm((CHIPS, SLOT, 2 * EA), BF),
            vm((11, SLOT, 2 * EA), BF),
            vm((4, SLOT, 2 * EA), BF),
            vm((4, SLOT, 2 * EA), BF),
            vm((CHIPS, SLOT, EB + 128), BF),
            vm((11, SLOT, EB + 128), BF),
            vm((4, SLOT, EB + 128), BF),
            vm((4, SLOT, EB + 128), BF),
            vm((SLOT, 128), F32),
            vm((CHIPS, SLOT, EA), BF),
            vm((CHIPS, SLOT, EB), BF),
            vm((2, 16, SLOT, WP), BF),
            vm((32, SLOT, WP), BF),
            dma((12,)),
            dma((N_SENT,)),
            dma((N_SENT,)),
            dma((9,)),
            dma((18,)),
        ],
        compiler_params=pltpu.CompilerParams(
            collective_id=0, has_side_effects=True, vmem_limit_bytes=56 * 1024 * 1024
        ),
    )(q, k, v, lens, wo, res, gain.reshape(1, W), ids, gw, wg, wu, wd)


def solution(mesh):
    in_specs = (
        P("rep", "attn", "ffn"),
        P("rep", "attn", None, None),
        P("rep", "attn", None, None),
        P("rep", "attn"),
        P("attn", "ffn"),
        P("rep", "ffn", "attn"),
        P("attn"),
        P("rep", "ffn", None),
        P("rep", "ffn", None),
        P("ffn", "attn", "rep"),
        P("ffn", "attn", "rep"),
        P("ffn", "attn", "rep"),
    )
    out_specs = P("rep", "ffn", "attn")
    return jax.shard_map(
        per_device, mesh=mesh, in_specs=in_specs, out_specs=out_specs, check_vma=False
    )
```

```python
import functools

import jax
import jax.numpy as jnp
from jax import lax
from jax.experimental import pallas as pl
from jax.experimental.pallas import tpu as pltpu
from jax.sharding import PartitionSpec as P

MESH = pl.DeviceIdType.MESH
BF = jnp.bfloat16
F32 = jnp.float32
NT = (((1,), (1,)), ((), ()))
NN = (((1,), (0,)), ((), ()))

CHIPS = 16
SIDE = 4
W = 224
WP = 256
CAP = 14
SLOT = 16
ROWS = 32
EFF = 640
EA, EB = 384, 256
TAIL = 512
HD = 256
KH = 2048
D = 7168

PLANE = sorted(
    ((df, dr, dc) for df in range(4) for dr in range(4) for dc in range(2) if df or dr or dc),
    key=lambda o: (-(min(o[0], 4 - o[0]) + min(o[1], 4 - o[1])), o),
)
XCORE = sorted(
    ((df, dc) for df in range(4) for dc in range(2) if df or dc),
    key=lambda o: (-min(o[0], 4 - o[0]), o),
)

FIRST = (0, 1, -1)
MIDDLE = (5, -5, 2, -2, 3, -3, 4, -4)
LAST = (6, -6, 7, -7, 8)
RELAY = {0: (5, 1), 1: (4, 3, 2), 5: (8, 7, 6)}


def mm(a, b, dims=NN):
    return lax.dot_general(a, b, dims, preferred_element_type=F32)


def kernel(
    q_h, k_h, v_h, len_h, wo_h, res_h, gain_h, ids_h, gw_h, wg_h, wu_h, wd_h,
    out_ref,
    qv, kv, vv, lenv, resv, gainv, idsv, gwv, wo, wg, wu, wd,
    qs, att, xs, xr, ag1, ag1b, us, rb, pad32, pad1, tok, xb, pb_a, r1_a, s2_a, r2_a, pb_b, r1_b, s2_b, r2_b, last_up, ag2_a, ag2_b, eb, rr,
    ld, ss, rs, out_s, in_s,
):
    a = lax.axis_index("attn")
    f = lax.axis_index("ffn")
    r = lax.axis_index("rep")
    c = lax.rem(a, 2)
    z = lax.div(a, 2)
    sg = 1 - 2 * c

    def zdev(d):
        return {"attn": lax.rem(z + d + CHIPS, CHIPS) * 2 + c}

    def zidx(d):
        return lax.rem(z + d + 2 * CHIPS, CHIPS)

    def pdev(o):
        df, dr, dc = o
        return {
            "attn": z * 2 + lax.rem(c + dc, 2),
            "ffn": lax.rem(f + df, 4),
            "rep": lax.rem(r + dr, 4),
        }

    sib = {"attn": z * 2 + 1 - c}

    loads = []

    def load(src, dst):
        cp = pltpu.make_async_copy(src, dst, ld.at[len(loads)])
        cp.start()
        loads.append(cp)
        return cp

    sent = []
    groups = {}

    def remote(src, dst, send_sem, recv_sem, dev):
        return pltpu.make_async_remote_copy(
            src_ref=src, dst_ref=dst, send_sem=send_sem, recv_sem=recv_sem,
            device_id=dev, device_id_type=MESH,
        )

    def send(src, dst, dev, group=None, arrival=None):
        k = len(sent)
        if group is None:
            leave = ss.at[k]
        else:
            groups[group] = groups.get(group, 0) + 1
            leave = out_s.at[group]
        cp = remote(src, dst, leave, rs.at[k] if arrival is None else in_s.at[arrival], dev)
        cp.start()
        sent.append((group, cp))
        return cp

    def wait_in(blocks, arrival):
        remote(blocks, blocks, out_s.at[0], in_s.at[arrival], sib).wait_recv()

    l_q = load(q_h.at[0], qv)
    l_k = load(k_h.at[0], kv)
    l_v = load(v_h.at[0], vv)
    l_len = load(len_h, lenv)

    barrier = pltpu.get_barrier_semaphore()
    peers = [zdev(d) for d in (5, -5)] + [pdev(o) for o in PLANE]
    peers += [zdev(d) for d in (3, -3, 2, -2, 1, -1)]
    for dev in peers:
        pl.semaphore_signal(barrier, inc=1, device_id=dev, device_id_type=MESH)

    l_ids = load(ids_h, idsv)
    l_gw = load(gw_h, gwv)
    l_res = load(res_h.at[0], resv)
    l_gain = load(gain_h, gainv)
    half = pl.multiple_of(c * KH, KH)
    other = pl.multiple_of((1 - c) * KH, KH)
    l_wo = load(wo_h.at[:, pl.ds(half, KH)], wo.at[c, pl.ds(0, W)])
    l_wg = load(wg_h.at[c], wg.at[c, pl.ds(0, W)])
    l_wu = load(wu_h.at[c], wu.at[c, pl.ds(0, W)])
    l_wd = load(wd_h.at[c], wd.at[c, pl.ds(0, W)])

    l_q.wait()
    q32 = qv[...].astype(F32)
    for i in range(4):
        for h in range(16):
            qs[i * 16 + h : i * 16 + h + 1, :] = q32[i : i + 1, h * HD : (h + 1) * HD]
    l_k.wait()
    l_len.wait()
    l_v.wait()
    position = lax.broadcasted_iota(jnp.int32, (16, HD), 1)
    for i in range(4):
        s = mm(qs[i * 16 : (i + 1) * 16, :].astype(BF), kv[i], NT) * (HD**-0.5)
        s = jnp.where(position < lenv[0:1, i : i + 1], s, F32(-1e30))
        e = jnp.exp(s - jnp.max(s, axis=1, keepdims=True))
        p = (e / jnp.sum(e, axis=1, keepdims=True)).astype(BF)
        o = mm(p, vv[i])
        for h in range(16):
            hh, hg, j = h // 8, (h % 8) // 4, h % 4
            for k in range(2):
                row = hg * 8 + k * 4 + i
                att[hh, row : row + 1, j * HD : (j + 1) * HD] = o[h : h + 1, :]
    rowi = lax.broadcasted_iota(jnp.int32, (16, 1024), 0)
    mine = lax.rem(lax.div(rowi, 4), 2) == c
    xs[...] = jnp.where(mine, att[1 - c], 0.0).astype(BF)

    pl.semaphore_wait(barrier, len(peers))
    x_cp = send(xs, xr, sib)

    def gather_z(buf, group):
        got = {}

        def pass_on(o):
            block = buf.at[zidx(-o)]
            for to in RELAY[abs(o)]:
                if o == 0:
                    got[to] = send(block, block, zdev(to), group)
                    got[-to] = send(block, block, zdev(-to), group)
                elif to < 8:
                    sgn = 1 if o > 0 else -1
                    arrival = 2 * group + (sgn * to in LAST)
                    send(block, block, zdev(sgn * to - o), group, arrival)

        pass_on(0)
        yield
        for sgn in (1, -1):
            got[sgn].wait_recv()
            pass_on(sgn)
        yield
        got[5].wait_recv()
        got[-5].wait_recv()
        far = buf.at[zidx(-5 * sg)]
        send(far, far, zdev(3 * sg), group, 2 * group + 1)
        pass_on(5)
        pass_on(-5)
        yield
        wait_in(buf.at[pl.ds(0, len(MIDDLE) - 2)], 2 * group)
        yield
        wait_in(buf.at[pl.ds(0, len(LAST))], 2 * group + 1)

    x_cp.wait_recv()
    whole_block = jnp.where(mine, att[c], 0.0).astype(BF) + xr[...]
    ag1[z] = whole_block[:, 0:512]
    ag1b[z] = whole_block[:, 512:1024]
    heads = gather_z(ag1, 0)
    heads_b = gather_z(ag1b, 8)
    next(heads)
    next(heads_b)
    x_wo = send(wo_h.at[:, pl.ds(other, KH)], wo.at[c, pl.ds(0, W)], sib)
    x_wg = send(wg_h.at[1 - c], wg.at[c, pl.ds(0, W)], sib)
    x_wu = send(wu_h.at[1 - c], wu.at[c, pl.ds(0, W)], sib)
    x_wd = send(wd_h.at[1 - c], wd.at[c, pl.ds(0, W)], sib)

    for buf in (wo, wg, wu, wd):
        buf[:, W:WP, :] = jnp.zeros((2, WP - W, buf.shape[2]), BF)
    l_res.wait()
    l_gain.wait()
    l_ids.wait()
    l_gw.wait()
    pad32[...] = jnp.zeros((ROWS, WP), F32)
    pad32[:, 0:W] = resv[...].astype(F32)
    pad1[...] = jnp.zeros((1, WP), F32)
    pad1[:, 0:W] = gainv[...]
    spot = lax.broadcasted_iota(jnp.int32, (128, ROWS), 0)
    hits = jnp.zeros((128, ROWS), F32)
    share = jnp.zeros((128, ROWS), F32)
    for k in range(3):
        same = idsv[k] == lax.div(spot, SLOT)
        hits = hits + jnp.where(same, 1.0, 0.0)
        share = share + jnp.where(same, gwv[k], 0.0)
    earlier = lax.broadcasted_iota(jnp.int32, (ROWS, ROWS), 0) < lax.broadcasted_iota(
        jnp.int32, (ROWS, ROWS), 1
    )
    before = mm(hits.astype(BF), jnp.where(earlier, 1.0, 0.0).astype(BF))
    placed = before == lax.rem(spot, SLOT).astype(F32)
    pick = jnp.where(placed, hits, 0.0).astype(BF)
    share = jnp.where(placed, share, 0.0)
    eye = lax.broadcasted_iota(jnp.int32, (ROWS, ROWS), 0) == lax.broadcasted_iota(
        jnp.int32, (ROWS, ROWS), 1
    )
    eye = jnp.where(eye, 1.0, 0.0).astype(BF)
    share_hi = share.astype(BF)
    share_lo = (share - share_hi.astype(F32)).astype(BF)
    share_hi = jnp.concatenate([mm(eye, share_hi, NT).astype(BF)] * 4, axis=1)
    share_lo = jnp.concatenate([mm(eye, share_lo, NT).astype(BF)] * 4, axis=1)


    for _ in range(2):
        next(heads)
        next(heads_b)
    for it in (heads, heads_b):
        for _ in it:
            pass
    l_wo.wait()
    x_wo.wait_recv()

    rows = ag1[...].reshape(CHIPS * 16, 512)
    rows_b = ag1b[...].reshape(CHIPS * 16, 512)
    for s in range(2):
        p0 = mm(rows, wo[s, :, 0:512], NT) + mm(rows_b, wo[s, :, 512:1024], NT)
        p1 = mm(rows, wo[s, :, 1024:1536], NT) + mm(rows_b, wo[s, :, 1536:2048], NT)
        p0, p1 = p0.reshape(CHIPS, 16, WP), p1.reshape(CHIPS, 16, WP)
        u = p0[:, 0:8] + p1[:, 8:16]
        us[s] = u.reshape(4, ROWS, WP).astype(BF)
    for df, dc in XCORE:
        q = lax.rem(f + df, 4)
        s = lax.rem(c + dc, 2)
        send(us.at[s, q], rb.at[f * 2 + c], pdev((df, 0, dc)), 3, 6)
    rb[f * 2 + c] = us[c, f]
    hidden = pad32[...]
    wait_in(rb.at[pl.ds(0, 7)], 6)
    for k in range(8):
        hidden = hidden + rb[k].astype(F32)
    hid = hidden.astype(BF).astype(F32)
    squares = jnp.sum(hid * hid, axis=1, keepdims=True)
    sq_hi = squares.astype(BF).astype(F32)
    lane2 = lax.broadcasted_iota(jnp.int32, (ROWS, WP), 1)
    normed = jnp.where(
        lane2 == W, sq_hi, jnp.where(lane2 == W + 1, squares - sq_hi, hid * pad1[...])
    ).astype(BF)
    tok[...] = mm(pick, normed).astype(BF).reshape(8, SLOT, WP)

    for o in PLANE:
        e = lax.rem(f + o[0], 4) * 2 + lax.rem(c + o[2], 2)
        send(tok.at[e], xb.at[c * 16 + r * 4 + f], pdev(o), 4, 7)
    xb[c * 16 + r * 4 + f] = tok[f * 2 + c]
    l_wg.wait()
    x_wg.wait_recv()
    l_wu.wait()
    x_wu.wait_recv()
    wait_in(xb.at[pl.ds(0, 31)], 7)
    x0 = xb[0:16].reshape(256, WP)
    x1 = xb[16:32].reshape(256, WP)
    ones = lax.broadcasted_iota(jnp.int32, (16, WP), 1)
    ones = jnp.where((ones == W) | (ones == W + 1), 1.0, 0.0).astype(BF)
    sq = (mm(ones, x0, NT) + mm(ones, x1, NT))[0:1, :]
    sq_hi = sq.astype(BF).astype(F32)
    sq_lo = sq - sq_hi
    def project(w, lo, hi):
        out = mm(x0, w[0, :, lo:hi]) + mm(x1, w[1, :, lo:hi])
        return out.reshape(CHIPS, SLOT, hi - lo)

    tail = project(wu, TAIL, EFF)
    slot = lax.broadcasted_iota(jnp.int32, (CHIPS, SLOT, 128), 1)

    def put(buf, column, base, first_tile):
        for j in range(base.shape[2] // 128):
            t = first_tile + j
            if t in (2, 3):
                low = sq_hi[:, (t - 2) * 128 : (t - 1) * 128].reshape(1, 1, 128)
            elif t in (4, 5):
                low = sq_lo[:, (t - 4) * 128 : (t - 3) * 128].reshape(1, 1, 128)
            else:
                k = 9 + t if t < 2 else 5 + t
                low = tail[:, k : k + 1, :]
            piece = jnp.where(slot == CAP + 1, low, base[:, :, j * 128 : (j + 1) * 128])
            piece = jnp.where(slot == CAP, tail[:, t : t + 1, :], piece)
            buf[:, :, column + j * 128 : column + (j + 1) * 128] = piece.astype(BF)

    sides = ((0, 1), (1, -1))

    class Sum:
        def __init__(self, pb, r1, s2, r2, group):
            self.pb, self.r1, self.s2, self.r2 = pb, r1, s2, r2
            self.group, self.arrival = group, 8 + 3 * (group - 5)

        def leaves(self):
            slots = ((7, -1, 0), (5, 1, 2), (8, 0, 4), (4, -2, 5), (3, -1, 7), (1, 1, 9))
            for o, d, k in slots:
                arrival = self.arrival + (k > 4)
                if o == 8:
                    send(self.pb.at[zidx(8)], self.r1.at[k], zdev(-2 * sg), self.group, arrival)
                    continue
                for side, sgn in sides:
                    src = self.pb.at[zidx(-sgn * o)]
                    send(src, self.r1.at[k + side], zdev(sgn * d), self.group, arrival)

        def relay(self, slot, o, first, last):
            wait_in(self.r1.at[pl.ds(first, last - first)], self.arrival + slot)
            for side, sgn in sides:
                acc = self.pb[zidx(-sgn * o)].astype(F32)
                for k in range(first + side, min(last, first + 4) if o == 6 else last, 2):
                    acc = acc + self.r1[k].astype(F32)
                if o == 6:
                    acc = acc + jnp.where(c == side, self.r1[4].astype(F32), 0.0)
                k = 2 * slot + side
                self.s2[k] = acc.astype(BF)
                send(self.s2.at[k], self.r2.at[k], zdev(-sgn * o), self.group, self.arrival + 2)

        def total(self):
            wait_in(self.r2, self.arrival + 2)
            out = self.pb[z].astype(F32)
            for k in range(4):
                out = out + self.r2[k].astype(F32)
            return out

    sum_a, sum_b = Sum(pb_a, r1_a, s2_a, r2_a, 5), Sum(pb_b, r1_b, s2_b, r2_b, 6)
    put(pb_a, 0, project(wg, 0, EA), 0)
    put(pb_a, EA, project(wu, 0, EA), 3)
    sum_a.leaves()
    put(pb_b, 0, project(wg, EA, EFF), 6)
    put(pb_b, EB, project(wu, EA, TAIL), 8)
    sum_b.leaves()
    sum_a.relay(0, 6, 0, 5)
    sum_b.relay(0, 6, 0, 5)
    sum_a.relay(1, 2, 5, 11)
    sum_b.relay(1, 2, 5, 11)

    def activate(gate, up):
        gate, up = gate * rinv, up * rinv
        act = gate / (1.0 + jnp.exp(-gate)) * up
        live = lax.broadcasted_iota(jnp.int32, act.shape, 0) < CAP
        return jnp.where(live, act, 0.0).astype(BF)

    total = sum_a.total()
    for t in range(6):
        last_up[t : t + 1, :] = total[CAP : CAP + 1, t * 128 : (t + 1) * 128]
    for t in range(2):
        last_up[9 + t : 10 + t, :] = total[CAP + 1 : CAP + 2, t * 128 : (t + 1) * 128]
    sq = total[CAP + 1 : CAP + 2, 256:512] + total[CAP + 1 : CAP + 2, 512:768]
    row = lax.broadcasted_iota(jnp.int32, (SLOT, 256), 0)
    lane3 = lax.broadcasted_iota(jnp.int32, (SLOT, 256), 1)
    sq = jnp.sum(jnp.where(lane3 == z * SLOT + row, sq, 0.0), axis=1, keepdims=True)
    rinv = lax.rsqrt(sq / D + 1e-6)
    ag2_a[z] = activate(total[:, 0:EA], total[:, EA : 2 * EA])
    rows_a = gather_z(ag2_a, 1)
    next(rows_a)
    total = sum_b.total()
    for t in range(3):
        last_up[6 + t : 7 + t, :] = total[CAP : CAP + 1, t * 128 : (t + 1) * 128]
        last_up[11 + t : 12 + t, :] = total[CAP + 1 : CAP + 2, t * 128 : (t + 1) * 128]
    last_up[CAP:SLOT, :] = jnp.zeros((SLOT - CAP, 128), F32)
    up = jnp.concatenate([total[:, EB : EB + 128], last_up[...]], axis=1)
    ag2_b[z] = activate(total[:, 0:EB], up)
    rows_b = gather_z(ag2_b, 2)
    next(rows_b)

    l_wd.wait()
    x_wd.wait_recv()
    me = r * 8 + f * 2 + c
    stay = []

    def give_back(offsets):
        first = len(stay)
        act_a = jnp.concatenate([ag2_a[zidx(-o)] for o in offsets], axis=0)
        act_b = jnp.concatenate([ag2_b[zidx(-o)] for o in offsets], axis=0)
        for s in range(2):
            out = mm(act_a, wd[s, :, 0:EA], NT) + mm(act_b, wd[s, :, EA:EFF], NT)
            eb[s, first : first + len(offsets)] = out.astype(BF).reshape(len(offsets), SLOT, WP)
        for k, o in enumerate(offsets):
            b = zidx(-o)
            fo, ro = lax.rem(b, 4), lax.div(b, 4)
            i = first + k
            stay.append(i)
            dev = {"attn": z * 2 + 1 - c, "ffn": fo, "rep": ro}
            send(eb.at[1 - c, i], rr.at[me], dev, 7, 14)
            away = b != r * 4 + f

            @pl.when(away)
            def _():
                dev = {"attn": z * 2 + c, "ffn": fo, "rep": ro}
                remote(eb.at[c, i], rr.at[me], out_s.at[7], in_s.at[14], dev).start()

            @pl.when(jnp.logical_not(away))
            def _():
                rr[me] = eb[c, i]

    next(rows_a)
    next(rows_b)
    next(rows_a)
    give_back(FIRST)
    next(rows_b)
    next(rows_a)
    next(rows_b)
    give_back(MIDDLE)
    for rows in (rows_a, rows_b):
        for _ in rows:
            pass
    give_back(LAST)
    wait_in(rr.at[pl.ds(0, 31)], 14)
    back = rr[...].reshape(512, WP)
    mixed = hidden + mm(share_hi, back) + mm(share_lo, back)
    out_ref[0] = mixed[:, 0:W]
    for group, cp in sent:
        if group is None:
            cp.wait_send()
    groups[7] = 31
    whole = {8: ag1b, 0: ag1, 1: ag2_a, 2: ag2_b, 3: rb, 4: xb, 5: pb_a, 6: pb_b, 7: rr}
    for group, n in groups.items():
        blocks = whole[group].at[pl.ds(0, n)]
        remote(blocks, blocks, out_s.at[group], in_s.at[0], sib).wait_send()


N_SENT = 5 + 30 + 7 + 31 + 30 + 30 + 16


def per_device(q, k, v, lens, wo, res, gain, ids, gw, wg, wu, wd):
    ids = jnp.transpose(ids, (2, 0, 1))
    gw = jnp.transpose(gw, (2, 0, 1))
    any_spec = pl.BlockSpec(memory_space=pl.ANY)
    vm = pltpu.VMEM
    dma = pltpu.SemaphoreType.DMA
    return pl.pallas_call(
        kernel,
        name="layer",
        out_shape=pltpu.VMEM((1, ROWS, W), F32),
        in_specs=[any_spec] * 12,
        out_specs=pl.BlockSpec(memory_space=pltpu.VMEM),
        scratch_shapes=[
            vm((4, 4096), BF),
            vm((4, 256, HD), BF),
            vm((4, 256, HD), BF),
            vm((1, 4), jnp.int32),
            vm((ROWS, W), BF),
            vm((1, W), F32),
            vm((3, 1, ROWS), jnp.int32),
            vm((3, 1, ROWS), F32),
            vm((2, WP, KH), BF),
            vm((2, WP, EFF), BF),
            vm((2, WP, EFF), BF),
            vm((2, WP, EFF), BF),
            vm((64, HD), F32),
            vm((2, 16, 1024), F32),
            vm((16, 1024), BF),
            vm((16, 1024), BF),
            vm((CHIPS, 16, 512), BF),
            vm((CHIPS, 16, 512), BF),
            vm((2, 4, ROWS, WP), BF),
            vm((8, ROWS, WP), BF),
            vm((ROWS, WP), F32),
            vm((1, WP), F32),
            vm((8, SLOT, WP), BF),
            vm((32, SLOT, WP), BF),
            vm((CHIPS, SLOT, 2 * EA), BF),
            vm((11, SLOT, 2 * EA), BF),
            vm((4, SLOT, 2 * EA), BF),
            vm((4, SLOT, 2 * EA), BF),
            vm((CHIPS, SLOT, EB + 128), BF),
            vm((11, SLOT, EB + 128), BF),
            vm((4, SLOT, EB + 128), BF),
            vm((4, SLOT, EB + 128), BF),
            vm((SLOT, 128), F32),
            vm((CHIPS, SLOT, EA), BF),
            vm((CHIPS, SLOT, EB), BF),
            vm((2, 16, SLOT, WP), BF),
            vm((32, SLOT, WP), BF),
            dma((12,)),
            dma((N_SENT,)),
            dma((N_SENT,)),
            dma((9,)),
            dma((18,)),
        ],
        compiler_params=pltpu.CompilerParams(
            collective_id=0, has_side_effects=True, vmem_limit_bytes=56 * 1024 * 1024
        ),
    )(q, k, v, lens, wo, res, gain.reshape(1, W), ids, gw, wg, wu, wd)


def solution(mesh):
    in_specs = (
        P("rep", "attn", "ffn"),
        P("rep", "attn", None, None),
        P("rep", "attn", None, None),
        P("rep", "attn"),
        P("attn", "ffn"),
        P("rep", "ffn", "attn"),
        P("attn"),
        P("rep", "ffn", None),
        P("rep", "ffn", None),
        P("ffn", "attn", "rep"),
        P("ffn", "attn", "rep"),
        P("ffn", "attn", "rep"),
    )
    out_specs = P("rep", "ffn", "attn")
    return jax.shard_map(
        per_device, mesh=mesh, in_specs=in_specs, out_specs=out_specs, check_vma=False
    )
```
